32 devices in a mesh: batch: 8 (over z, x), seq: 4 (over y, core).
Axes of the slice: x: 2, y: 2, z: 4, core: 2. Of those that a mesh axis runs over, the one named last changes fastest.
Arguments:
- tokens: bfloat16 [8, 2048, 512], P('batch', 'seq'), may hold values from -6 to 6
- prefix: int32 [8], P('batch'), may hold values from 0 to 1023
- cotangent: bfloat16 [8, 2048, 512], P('batch', 'seq'), may hold values from -6 to 6
- ln1_gain: bfloat16 [512], replicated, may hold values from 0.25 to 1.75
- ln1_bias: bfloat16 [512], replicated, may hold values from -1.5 to 1.5
- w_qkv: bfloat16 [512, 1536], replicated, may hold values from -0.25 to 0.25
- w_out: bfloat16 [512, 512], replicated, may hold values from -1 to 1
- ln2_gain: bfloat16 [512], replicated, may hold values from 0.25 to 1.75
- ln2_bias: bfloat16 [512], replicated, may hold values from -1.5 to 1.5
- w_up: bfloat16 [512, 2048], replicated, may hold values from -0.25 to 0.25
- w_down: bfloat16 [2048, 512], replicated, may hold values from -0.125 to 0.125
Outputs:
- output: bfloat16 [8, 2048, 512], P('batch', 'seq')
- grad_tokens: bfloat16 [8, 2048, 512], P('batch', 'seq')
- grad_ln1_gain: float32 [512], replicated
- grad_ln1_bias: float32 [512], replicated
- grad_w_qkv: float32 [512, 1536], replicated
- grad_w_out: float32 [512, 512], replicated
- grad_ln2_gain: float32 [512], replicated
- grad_ln2_bias: float32 [512], replicated
- grad_w_up: float32 [512, 2048], replicated
- grad_w_down: float32 [2048, 512], replicated
The draws below stay inside these ranges and needn't reach their ends.
All inputs are finite; a program needn't handle non-finite values.
Results may differ from the reference program's by a relative error of at most 0.011.
Values may be sent and summed in bfloat16 or wider, within the bound.
No kernel may reach another device: no remote copies, remote signals or barrier semaphores. Data moves between devices by JAX's collectives and lax.ppermute only.
A program may use at most 128 MiB of HBM per device.

```python
import math
import jax
import jax.numpy as jnp
from jax import lax

D = 512
HEADS = 8
HEAD = 64
FF = 2048
BLOCK = 16
LEVELS = 6
SEQLEN = 2048
ROWS = 8


def set_ends(values, own_key, low, high):
    longest = values.shape.index(max(values.shape))
    spots = []
    for shift in (0, 1):
        where = [jax.random.randint(jax.random.fold_in(own_key, axis), (), 0, length) for axis, length in enumerate(values.shape)]
        where[longest] = (where[longest] + shift) % values.shape[longest]
        spots.append(tuple(where))
    return values.at[spots[0]].set(low).at[spots[1]].set(high)


def level_of(stream_key, shape, shards, least, high):
    gain = 1.0
    for dim, shards_of in shards:
        draws = jax.random.uniform(jax.random.fold_in(jax.random.fold_in(stream_key, 6), dim), (shards_of,), jnp.float32, least / len(shards), high / len(shards))
        gain = gain * jnp.repeat(jnp.exp(draws), shape[dim] // shards_of).reshape((-1,) + (1,) * (len(shape) - 1 - dim))
    return gain


def bell_draw(rng, dims, deviation, limit, pieces=(), kind=jnp.bfloat16):
    factor_of = level_of(rng, dims, pieces, -0.22, 0.18) if pieces else 1.0
    drawn = jax.random.normal(rng, dims, jnp.float32) * deviation * factor_of
    return jnp.minimum(jnp.maximum(drawn, -limit), limit).astype(kind)


def setup_inputs(seed: int = 0) -> dict:
    keys = jax.random.split(jax.random.key(seed), 12)
    return {
        "tokens": bell_draw(keys[0], (ROWS, SEQLEN, D), 1.0, 6.0, ((0, 8), (1, 4))),
        "prefix": set_ends(jax.random.randint(keys[1], (ROWS,), 0, SEQLEN // 2), jax.random.fold_in(keys[1], 1), 0, (SEQLEN // 2) - 1).astype(jnp.int32),
        "cotangent": bell_draw(keys[2], (ROWS, SEQLEN, D), 1.0, 6.0, ((0, 8), (1, 4))),
        "ln1_gain": jnp.clip(1.0 + 0.15 * jax.random.normal(keys[3], (D,), jnp.float32), 0.25, 1.75).astype(jnp.bfloat16),
        "ln1_bias": bell_draw(keys[4], (D,), 0.3, 1.5),
        "w_qkv": bell_draw(keys[5], (D, 3 * D), D ** -0.5, 0.25),
        "w_out": bell_draw(keys[6], (D, D), (D // 16) ** -0.5, 1.0),
        "ln2_gain": jnp.clip(1.0 + 0.15 * jax.random.normal(keys[7], (D,), jnp.float32), 0.25, 1.75).astype(jnp.bfloat16),
        "ln2_bias": bell_draw(keys[8], (D,), 0.3, 1.5),
        "w_up": bell_draw(keys[9], (D, FF), D ** -0.5, 0.25),
        "w_down": bell_draw(keys[10], (FF, D), FF ** -0.5, 0.125),
    }


@jax.custom_vjp
def low(v):
    return lax.optimization_barrier(v.astype(jnp.bfloat16)).astype(jnp.float32)

@jax.custom_vjp
def low_back(v):
    return v

def low_keep(v):
    return (low(v), None)

def low_pass(kept, grad):
    return (grad,)

def back_keep(v):
    return (v, None)

def back_low(kept, grad):
    return (low(grad),)
low.defvjp(low_keep, low_pass)
low_back.defvjp(back_keep, back_low)

def layer_norm(values, gain_vec, bias_vec):
    average = lax.optimization_barrier(jnp.mean(values, axis=-1, keepdims=True))
    centred = values - average
    variance = lax.optimization_barrier(jnp.mean(centred * centred, axis=-1, keepdims=True))
    return centred * lax.rsqrt(variance + 1e-05) * gain_vec + bias_vec

def level_masks(positions, level_idx):
    group_size = 2 ** level_idx
    offsets = jnp.arange(2 * BLOCK, dtype=jnp.int32)
    coarse_idx = (positions[:, None] // (BLOCK * group_size) - 1) * BLOCK + offsets[None, :]
    if level_idx == 0:
        return (coarse_idx >= 0) & (coarse_idx <= positions[:, None])
    half_block = BLOCK // 2 * group_size
    finer_start = (positions[:, None] // half_block - 1) * half_block
    return (coarse_idx >= 0) & ((coarse_idx + 1) * group_size <= finer_start)

def windows(full_seq, span_len, group_size):
    lead_dims = full_seq.shape[:-2]
    blocks = span_len // (BLOCK * group_size)
    win_shape = lead_dims + (blocks, BLOCK, HEADS, full_seq.shape[-1] // HEADS)
    earlier = full_seq[..., :-BLOCK, :].reshape(win_shape)
    later = full_seq[..., BLOCK:, :].reshape(win_shape)
    return jnp.concatenate([earlier, later], axis=len(lead_dims) + 1)

def row_forward(inputs, ln1_gain, ln1_bias, w_qkv, w_out, ln2_gain, ln2_bias, w_up, w_down):
    precise = lax.Precision.HIGHEST
    normed = low(layer_norm(inputs, ln1_gain, ln1_bias))
    projected = low(low_back(jnp.dot(normed, w_qkv, precision=precise)))
    queries = projected[:, :D]
    key_rows = projected[:, D:2 * D]
    value_rows = projected[:, 2 * D:]
    positions = jnp.arange(SEQLEN, dtype=jnp.int32)
    score_scale = 1.0 / math.sqrt(HEAD)
    score_parts = []
    value_wins = []
    for level_idx in range(LEVELS):
        group_size = 2 ** level_idx
        blocks = SEQLEN // (BLOCK * group_size)
        if level_idx == 0:
            coarse_k = key_rows
            coarse_v = value_rows
        else:
            coarse_k = low(low_back(lax.optimization_barrier(jnp.mean(key_rows.reshape(SEQLEN // group_size, group_size, D), axis=1))))
            coarse_v = low(low_back(lax.optimization_barrier(jnp.mean(value_rows.reshape(SEQLEN // group_size, group_size, D), axis=1))))
        padding = jnp.zeros((BLOCK, D), jnp.float32)
        key_win = windows(jnp.concatenate([padding, coarse_k], axis=0), SEQLEN, group_size)
        value_wins.append(windows(jnp.concatenate([padding, coarse_v], axis=0), SEQLEN, group_size))
        query_blk = queries.reshape(blocks, BLOCK * group_size, HEADS, HEAD)
        raw_scores = jnp.einsum('bqhd,bkhd->bqhk', query_blk, key_win, precision=precise)
        raw_scores = raw_scores.reshape(SEQLEN, HEADS, 2 * BLOCK) * score_scale + math.log(group_size)
        score_parts.append(jnp.where(level_masks(positions, level_idx)[:, None, :], raw_scores, -1e+30))
    scores = low_back(jnp.concatenate(score_parts, axis=-1))
    soft_probs = low(jax.nn.softmax(scores, axis=-1))
    attended = jnp.zeros((SEQLEN, D), jnp.float32)
    for level_idx in range(LEVELS):
        group_size = 2 ** level_idx
        blocks = SEQLEN // (BLOCK * group_size)
        prob_part = soft_probs[:, :, 2 * BLOCK * level_idx:2 * BLOCK * (level_idx + 1)]
        prob_part = prob_part.reshape(blocks, BLOCK * group_size, HEADS, 2 * BLOCK)
        mixed = jnp.einsum('bqhk,bkhd->bqhd', prob_part, value_wins[level_idx], precision=precise)
        attended = attended + mixed.reshape(SEQLEN, D)
    attended = low(low_back(attended))
    mid = inputs + low_back(jnp.dot(attended, w_out, precision=precise))
    normed2 = low(layer_norm(mid, ln2_gain, ln2_bias))
    up_proj = low_back(jnp.dot(normed2, w_up, precision=precise))
    hidden = low(jax.nn.gelu(up_proj, approximate=True))
    return mid + low_back(jnp.dot(hidden, w_down, precision=precise))

def reference(tokens, prefix, cotangent, ln1_gain, ln1_bias, w_qkv, w_out, ln2_gain, ln2_bias, w_up, w_down):
    params = tuple((p.astype(jnp.float32) for p in (ln1_gain, ln1_bias, w_qkv, w_out, ln2_gain, ln2_bias, w_up, w_down)))
    positions = jnp.arange(SEQLEN, dtype=jnp.int32)

    def one_row(carry, row_data):
        token_row, cot_row, row_prefix = row_data
        scored = (positions >= row_prefix)[:, None]
        result, pull = jax.vjp(row_forward, token_row.astype(jnp.float32), *params)
        grads = pull(jnp.where(scored, cot_row.astype(jnp.float32), 0.0))
        new_carry = tuple((c + g for c, g in zip(carry, grads[1:])))
        return (new_carry, (result.astype(jnp.bfloat16), grads[0].astype(jnp.bfloat16)))
    init = tuple((jnp.zeros_like(p) for p in params))
    sums, outs = lax.scan(one_row, init, (tokens, cotangent, prefix))
    return (outs[0], outs[1], sums[0], sums[1], sums[2], sums[3], sums[4], sums[5], sums[6], sums[7])
```

```python
from functools import partial
import math

import jax
import jax.numpy as jnp
from jax import lax
from jax.experimental import pallas as pl
from jax.experimental.pallas import tpu as pltpu
from jax.sharding import PartitionSpec as P

HEADS = 8
BLOCK = 16
LEVELS = 6
CHUNK = 32
KEYS = 128
f32 = jnp.float32
bf16 = jnp.bfloat16


def nn(a, b):
    return lax.dot_general(a, b, (((1,), (0,)), ((), ())), preferred_element_type=f32)


def nt(a, b):
    return lax.dot_general(a, b, (((1,), (1,)), ((), ())), preferred_element_type=f32)


def tn(a, b):
    return lax.dot_general(a, b, (((0,), (0,)), ((), ())), preferred_element_type=f32)


def call(kernel, outs, *args, scratch=(), smem=(), name=None, flops=0, limit=40):
    specs = [
        pl.BlockSpec(memory_space=pltpu.SMEM if i in smem else pltpu.VMEM) for i in range(len(args))
    ]
    return pl.pallas_call(
        kernel,
        out_shape=[jax.ShapeDtypeStruct(s, d) for s, d in outs],
        in_specs=specs,
        out_specs=[pl.BlockSpec(memory_space=pltpu.VMEM)] * len(outs),
        scratch_shapes=scratch,
        compiler_params=pltpu.CompilerParams(vmem_limit_bytes=limit * 2**20),
        cost_estimate=pl.CostEstimate(flops=flops, bytes_accessed=2**20, transcendentals=0),
        name=name,
    )(*args)


def level_start(span, level):
    return span - (span >> (level - 1)) if level else 0


def unit(values):
    centred = values - jnp.mean(values, axis=-1, keepdims=True)
    inv = lax.rsqrt(jnp.mean(centred * centred, axis=-1, keepdims=True) + 1e-05)
    return centred * inv, inv


def unit_back(grad, hat, inv):
    along = jnp.mean(grad * hat, axis=-1, keepdims=True)
    return inv * (grad - jnp.mean(grad, axis=-1, keepdims=True) - hat * along)


def pool_matrix(span):
    parts = []
    for level in range(1, LEVELS):
        rows = span >> level
        row = lax.broadcasted_iota(jnp.int32, (rows, span), 0)
        col = lax.broadcasted_iota(jnp.int32, (rows, span), 1)
        parts.append(jnp.where((col >> level) == row, 1.0 / 2**level, 0.0))
    return jnp.concatenate(parts, axis=0).astype(bf16)


def project_kv(tokens, gain, bias, w_qkv, normed, kv, coarse, edge):
    span, width = tokens.shape
    hat, _ = unit(tokens[...].astype(f32))
    rows = (hat * gain[...].astype(f32) + bias[...].astype(f32)).astype(bf16)
    normed[...] = rows
    both = nn(rows, w_qkv[:, width:]).astype(bf16)
    kv[...] = both
    pooled = nn(pool_matrix(span), both).astype(bf16)
    coarse[...] = pooled
    edge[0:BLOCK] = both[span - BLOCK :]
    for level in range(1, LEVELS):
        end = level_start(span, level + 1)
        edge[BLOCK * level : BLOCK * (level + 1)] = pooled[end - BLOCK : end]


def project_q(place, normed, w_qkv, cotangent, w_down, queries, d_ffn, d_hidden):
    span, width = normed.shape
    q = nn(normed[...], w_qkv[:, :width]).astype(bf16).astype(f32)
    queries[...] = (q * (1.0 / math.sqrt(width // HEADS))).astype(bf16)
    position = place[0] * span + lax.broadcasted_iota(jnp.int32, (span, width), 0)
    masked = jnp.where(position >= place[2], cotangent[...].astype(f32), 0.0).astype(bf16)
    d_ffn[...] = masked
    d_hidden[...] = nt(masked, w_down[...])


def window_bias(chunk, first):
    row = lax.broadcasted_iota(jnp.int32, (CHUNK, KEYS), 0)
    col = lax.broadcasted_iota(jnp.int32, (CHUNK, KEYS), 1)
    late = row >= BLOCK
    low = jnp.where(late, BLOCK, 0)
    edge = 3 * BLOCK
    ok = (col >= low) & (col <= BLOCK + row)
    if chunk == 0:
        ok = ok & ((col >= BLOCK) | jnp.logical_not(first))
    bias = jnp.where(ok & (col < edge), 0.0, -1e30)
    for level in range(1, LEVELS):
        start = edge + BLOCK * (level - 1)
        inside = (col >= start) & (col < start + BLOCK)
        half = inside & (col < start + BLOCK // 2)
        if level == 1:
            ok = half | (inside & late)
        else:
            ok = inside if (chunk >> (level - 2)) & 1 else half
        if chunk >> (level - 1) == 0:
            ok = ok & jnp.logical_not(first)
        bias = jnp.where(ok, math.log(2**level), bias)
    return bias


def window_rows(kv, coarse, recv, chunk, low, high, span):
    start = CHUNK * chunk
    if chunk == 0:
        parts = [recv[0:BLOCK, low:high], kv[0:CHUNK, low:high]]
    else:
        parts = [kv[start - BLOCK : start + CHUNK, low:high]]
    for level in range(1, LEVELS):
        block = chunk >> (level - 1)
        if block == 0:
            parts.append(recv[BLOCK * level : BLOCK * (level + 1), low:high])
        else:
            base = level_start(span, level) + BLOCK * (block - 1)
            parts.append(coarse[base : base + BLOCK, low:high])
    return jnp.concatenate(parts, axis=0)


def by_head(rows):
    lane = lax.broadcasted_iota(jnp.int32, (CHUNK, 128), 1)
    zero = jnp.zeros((CHUNK, 128), bf16)
    pairs = []
    for pair in range(HEADS // 2):
        part = rows[:, 128 * pair : 128 * (pair + 1)]
        pairs.append(
            jnp.concatenate(
                [jnp.where(lane < 64, part, zero), jnp.where(lane >= 64, part, zero)], axis=0
            )
        )
    return pairs


def from_heads(pairs):
    lane = lax.broadcasted_iota(jnp.int32, (CHUNK, 128), 1)
    return jnp.concatenate([jnp.where(lane < 64, p[:CHUNK], p[CHUNK:]) for p in pairs], axis=1)


def attend(place, queries, kv, coarse, recv, attended, probs):
    span, width = queries.shape
    first = place[0] == 0
    rows = CHUNK * HEADS
    for chunk in range(span // CHUNK):
        start = CHUNK * chunk
        bias = window_bias(chunk, first)
        keys = window_rows(kv, coarse, recv, chunk, 0, width, span)
        vals = window_rows(kv, coarse, recv, chunk, width, 2 * width, span)
        split = by_head(queries[start : start + CHUNK])
        raw = [nt(s, keys[:, 128 * p : 128 * (p + 1)]) for p, s in enumerate(split)]
        scores = jnp.concatenate(raw, axis=0) + jnp.concatenate([bias] * HEADS, axis=0)
        expo = jnp.exp(scores - jnp.max(scores, axis=-1, keepdims=True))
        soft = expo / jnp.sum(expo, axis=-1, keepdims=True)
        low = soft.astype(bf16)
        probs[rows * chunk : rows * (chunk + 1)] = low
        mixed = [
            nn(low[64 * p : 64 * (p + 1)], vals[:, 128 * p : 128 * (p + 1)])
            for p in range(HEADS // 2)
        ]
        attended[start : start + CHUNK] = from_heads(mixed).astype(bf16)


def halves(whole, keep, send, core):
    rows = keep.shape[0]
    keep[...] = whole[pl.ds(core * rows, rows)]
    send[...] = whole[pl.ds((1 - core) * rows, rows)]


def feed_forward(
    attended, tokens, w_out, gain, bias, w_up, d_hidden, d_ffn, place, mid, normed, hidden, d_up, keep, send, whole
):
    span, width = tokens.shape
    ff = w_up.shape[1]
    middle = tokens[...].astype(f32) + nn(attended[...], w_out[...])
    mid[...] = middle
    hat, _ = unit(middle)
    rows = (hat * gain[...].astype(f32) + bias[...].astype(f32)).astype(bf16)
    normed[...] = rows
    c0 = math.sqrt(2.0 / math.pi)
    tile = 256
    for start in range(0, ff, tile):
        cols = slice(start, start + tile)
        x = nn(rows, w_up[:, cols])
        square = x * x
        half = 0.5 + 0.5 * jnp.tanh(x * (c0 + (c0 * 0.044715) * square))
        act = (x * half).astype(bf16)
        slope = half + 2.0 * half * (1.0 - half) * x * (c0 + (3 * c0 * 0.044715) * square)
        hidden[:, cols] = act
        d_up[:, cols] = (slope * d_hidden[:, cols]).astype(bf16)
        whole[cols] = tn(act, d_ffn[...]).astype(bf16)
    halves(whole, keep, send, place[1])


def up_back(normed, d_up, place, keep, send, whole):
    width = normed.shape[1]
    for part in range(d_up.shape[1] // width):
        cols = slice(width * part, width * (part + 1))
        whole[cols] = tn(normed[...], d_up[:, cols]).astype(bf16)
    halves(whole, keep, send, place[1])


def mid_back(
    mid, hidden, w_down, d_up, w_up, gain, d_ffn, attended, w_out, out, d_mid, d_attended, grad_out, grad_norm
):
    middle = mid[...]
    out[...] = (middle + nn(hidden[...], w_down[...])).astype(bf16)
    d_normed = nt(d_up[...], w_up[...])
    hat, inv = unit(middle)
    grad_norm[0:1] = jnp.sum(d_normed * hat, axis=0, keepdims=True)
    grad_norm[1:2] = jnp.sum(d_normed, axis=0, keepdims=True)
    d_middle = d_ffn[...].astype(f32) + unit_back(d_normed * gain[...].astype(f32), hat, inv)
    d_mid[...] = d_middle
    d_branch = d_middle.astype(bf16)
    grad_out[...] = tn(attended[...], d_branch).astype(bf16)
    d_attended[...] = nt(d_branch, w_out[...]).astype(bf16)


def attend_back(queries, kv, coarse, recv, probs, d_attended, d_queries, fine, wide, lent):
    span, width = queries.shape
    rows = CHUNK * HEADS
    scale = 1.0 / math.sqrt(width // HEADS)
    fine[...] = jnp.zeros_like(fine)
    wide[...] = jnp.zeros_like(wide)
    zero = jnp.zeros((2 * CHUNK, 128), bf16)
    for chunk in range(span // CHUNK):
        start = CHUNK * chunk
        keys = window_rows(kv, coarse, recv, chunk, 0, width, span)
        vals = window_rows(kv, coarse, recv, chunk, width, 2 * width, span)
        split_q = by_head(queries[start : start + CHUNK])
        split_a = by_head(d_attended[start : start + CHUNK])
        low = probs[rows * chunk : rows * (chunk + 1)]
        soft = low.astype(f32)
        d_probs = jnp.concatenate(
            [nt(s, vals[:, 128 * p : 128 * (p + 1)]) for p, s in enumerate(split_a)], axis=0
        )
        inner = jnp.sum(soft * d_probs, axis=-1, keepdims=True)
        d_scores = (soft * (d_probs - inner)).astype(bf16)
        mixed = [
            nn(d_scores[64 * p : 64 * (p + 1)], keys[:, 128 * p : 128 * (p + 1)])
            for p in range(HEADS // 2)
        ]
        d_queries[start : start + CHUNK] = (from_heads(mixed) * scale).astype(bf16)
        for part, (left, split) in enumerate(((d_scores, split_q), (low, split_a))):
            for quad in range(HEADS // 4):
                pair = 2 * quad
                right = jnp.concatenate(
                    [
                        jnp.concatenate([split[pair], zero], axis=1),
                        jnp.concatenate([zero, split[pair + 1]], axis=1),
                    ],
                    axis=0,
                )
                grad = tn(left[128 * quad : 128 * (quad + 1)], right)
                cols = slice(width * part + 256 * quad, width * part + 256 * (quad + 1))
                fine[start : start + 3 * BLOCK, cols] += grad[: 3 * BLOCK]
                for level in range(1, LEVELS):
                    base = level_start(span, level) + BLOCK * (chunk >> (level - 1))
                    at = BLOCK * (level + 2)
                    wide[base : base + BLOCK, cols] += grad[at : at + BLOCK]
    lent[0:BLOCK] = fine[0:BLOCK].astype(bf16)
    for level in range(1, LEVELS):
        base = level_start(span, level)
        lent[BLOCK * level : BLOCK * (level + 1)] = wide[base : base + BLOCK].astype(bf16)


def project_back(
    fine, wide, back, d_queries, normed, w_qkv, tokens, gain, d_mid, grad_out, grad_norm, place,
    d_tokens, keep, send, d_proj, whole,
):
    span, width = tokens.shape
    parts = []
    for level in range(1, LEVELS):
        base, end = level_start(span, level), level_start(span, level + 1)
        if base + BLOCK < end:
            parts.append(wide[base + BLOCK : end].astype(bf16))
        parts.append(back[BLOCK * level : BLOCK * (level + 1)])
    spread = tn(pool_matrix(span), jnp.concatenate(parts, axis=0))
    d_proj[:, :width] = d_queries[...]
    body = span - BLOCK
    d_proj[:body, width:] = (fine[BLOCK:span] + spread[:body]).astype(bf16)
    d_proj[body:, width:] = (
        fine[span:] + back[0:BLOCK].astype(f32) + spread[body:]
    ).astype(bf16)
    grads = d_proj[...]
    whole[:, : 3 * width] = tn(normed[...], grads).astype(bf16)
    whole[:, 3 * width : 4 * width] = grad_out[...]
    d_normed = nt(grads, w_qkv[...])
    hat, inv = unit(tokens[...].astype(f32))
    d_tokens[...] = (
        d_mid[...] + unit_back(d_normed * gain[...].astype(f32), hat, inv)
    ).astype(bf16)
    rows = [
        jnp.sum(d_normed * hat, axis=0, keepdims=True),
        jnp.sum(d_normed, axis=0, keepdims=True),
        grad_norm[0:2],
        jnp.zeros((124, width), f32),
    ]
    whole[:, 4 * width :] = jnp.concatenate(rows, axis=0).T.astype(bf16)
    halves(whole, keep, send, place[1])


def flips(size, bit):
    return [(i, i ^ (1 << bit)) for i in range(size)]


def reduce_scatter(keep, send, orders, index, size):
    axes = ("batch", "seq")
    own = keep.astype(f32) + lax.ppermute(send, axes, flips(size, 0)).astype(f32)
    own = own.astype(bf16)
    for even, odd in zip(*orders):
        rows = own.shape[0] // 2
        bit = jnp.where(index & 1, (index >> odd) & 1, (index >> even) & 1)
        pairs = [(i, i ^ (1 << (odd if i & 1 else even))) for i in range(size)]
        away = lax.dynamic_slice_in_dim(own, (1 - bit) * rows, rows, 0)
        here = lax.dynamic_slice_in_dim(own, bit * rows, rows, 0)
        own = (here.astype(f32) + lax.ppermute(away, axes, pairs).astype(f32)).astype(bf16)
    return own


def all_gather(own, orders, index, size):
    axes = ("batch", "seq")
    steps = [(0, 0)] + list(zip(*orders))
    for even, odd in reversed(steps):
        bit = jnp.where(index & 1, (index >> odd) & 1, (index >> even) & 1)
        pairs = [(i, i ^ (1 << (odd if i & 1 else even))) for i in range(size)]
        other = lax.ppermute(own, axes, pairs)
        own = jnp.where(
            bit == 0, jnp.concatenate([own, other], 0), jnp.concatenate([other, own], 0)
        )
    return own


def body(
    tokens, prefix, cotangent, ln1_gain, ln1_bias, w_qkv, w_out, ln2_gain, ln2_bias, w_up, w_down
):
    row_count, span, width = tokens.shape
    ff = w_up.shape[1]
    seq_size, batch_size = lax.axis_size("seq"), lax.axis_size("batch")
    size = seq_size * batch_size
    seq_at = lax.axis_index("seq")
    index = lax.axis_index("batch") * seq_size + seq_at
    place = jnp.stack([seq_at, index & 1, prefix[0], prefix[0]]).astype(jnp.int32)
    tokens = tokens.reshape(span, width)
    cotangent = cotangent.reshape(span, width)
    gain1, bias1, gain2, bias2 = (
        v.reshape(1, width) for v in (ln1_gain, ln1_bias, ln2_gain, ln2_bias)
    )
    edge_rows = BLOCK * LEVELS
    coarse_rows = level_start(span, LEVELS)
    normed1, kv, coarse, edge = call(
        project_kv,
        [((span, width), bf16), ((span, 2 * width), bf16), ((coarse_rows, 2 * width), bf16), ((edge_rows, 2 * width), bf16)],
        tokens, gain1, bias1, w_qkv,
        name="project_kv",
    )
    onward = [(i, i + 1) for i in range(seq_size - 1)]
    recv = lax.ppermute(edge, "seq", onward)
    queries, d_ffn, d_hidden = call(
        project_q,
        [((span, width), bf16), ((span, width), bf16), ((span, ff), f32)],
        place, normed1, w_qkv, cotangent, w_down,
        smem=(0,), name="project_q",
    )
    attended, probs = call(
        attend,
        [((span, width), bf16), ((span * HEADS, KEYS), bf16)],
        place, queries, kv, coarse, recv,
        smem=(0,), name="attend",
    )
    mid, normed2, hidden, d_up, keep_down, send_down = call(
        feed_forward,
        [((span, width), f32), ((span, width), bf16), ((span, ff), bf16), ((span, ff), bf16),
         ((ff // 2, width), bf16), ((ff // 2, width), bf16)],
        attended, tokens, w_out, gain2, bias2, w_up, d_hidden, d_ffn, place,
        smem=(8,), scratch=[pltpu.VMEM((ff, width), bf16)], name="feed_forward",
    )
    keep_up, send_up = call(
        up_back,
        [((ff // 2, width), bf16), ((ff // 2, width), bf16)],
        normed2, d_up, place,
        smem=(2,), scratch=[pltpu.VMEM((ff, width), bf16)], name="up_back",
    )
    out, d_mid, d_attended, grad_out, grad_norm = call(
        mid_back,
        [((span, width), bf16), ((span, width), f32), ((span, width), bf16), ((width, width), bf16), ((8, width), f32)],
        mid, hidden, w_down, d_up, w_up, gain2, d_ffn, attended, w_out,
        name="mid_back",
    )
    d_queries, fine, wide, lent = call(
        attend_back,
        [((span, width), bf16), ((span + BLOCK, 2 * width), f32), ((coarse_rows, 2 * width), f32), ((edge_rows, 2 * width), bf16)],
        queries, kv, coarse, recv, probs, d_attended,
        name="attend_back",
    )
    back = lax.ppermute(lent, "seq", [(b, a) for a, b in onward])
    d_tokens, keep_qkv, send_qkv = call(
        project_back,
        [((span, width), bf16), ((width // 2, 4 * width + 128), bf16), ((width // 2, 4 * width + 128), bf16)],
        fine, wide, back, d_queries, normed1, w_qkv, tokens, gain1, d_mid, grad_out, grad_norm, place,
        smem=(11,),
        scratch=[pltpu.VMEM((span, 3 * width), bf16), pltpu.VMEM((width, 4 * width + 128), bf16)],
        name="project_back",
    )
    bits = range(1, size.bit_length() - 1)
    orders = (list(bits), [2, 1] + list(bits)[2:])
    down = all_gather(reduce_scatter(keep_down, send_down, orders, index, size), orders, index, size)
    up = all_gather(reduce_scatter(keep_up, send_up, orders, index, size), orders, index, size)
    rest = all_gather(reduce_scatter(keep_qkv, send_qkv, orders, index, size), orders, index, size)
    parts = up.shape[0] // width
    up = jnp.concatenate([up[width * i : width * (i + 1)] for i in range(parts)], axis=1)
    small = rest[:, 4 * width :].astype(f32)
    return (
        out.reshape(row_count, span, width),
        d_tokens.reshape(row_count, span, width),
        small[:, 0],
        small[:, 1],
        rest[:, : 3 * width].astype(f32),
        rest[:, 3 * width : 4 * width].astype(f32),
        small[:, 2],
        small[:, 3],
        up.astype(f32),
        down.astype(f32),
    )


def solution(mesh):
    placed = (
        P("batch", "seq", None),
        P("batch"),
        P("batch", "seq", None),
        P(),
        P(),
        P(),
        P(),
        P(),
        P(),
        P(),
        P(),
    )
    return jax.shard_map(
        body,
        mesh=mesh,
        in_specs=placed,
        out_specs=(
            P("batch", "seq", None),
            P("batch", "seq", None),
            P(),
            P(),
            P(),
            P(),
            P(),
            P(),
            P(),
            P(),
        ),
        check_vma=False,
    )
```

```python
from functools import partial
import math

import jax
import jax.numpy as jnp
from jax import lax
from jax.experimental import pallas as pl
from jax.experimental.pallas import tpu as pltpu
from jax.sharding import PartitionSpec as P

HEADS = 8
BLOCK = 16
LEVELS = 6
CHUNK = 32
KEYS = 128
f32 = jnp.float32
bf16 = jnp.bfloat16


def nn(a, b):
    return lax.dot_general(a, b, (((1,), (0,)), ((), ())), preferred_element_type=f32)


def nt(a, b):
    return lax.dot_general(a, b, (((1,), (1,)), ((), ())), preferred_element_type=f32)


def tn(a, b):
    return lax.dot_general(a, b, (((0,), (0,)), ((), ())), preferred_element_type=f32)


def call(kernel, outs, *args, scratch=(), smem=(), far=(), far_out=(), deps=(), name=None, us=0.5, limit=8):
    def spec(at, apart):
        return pl.BlockSpec(memory_space=pltpu.HBM if at in apart else pltpu.VMEM)

    specs = [
        pl.BlockSpec(memory_space=pltpu.SMEM) if i in smem else spec(i, far) for i in range(len(args))
    ]
    specs += [pl.BlockSpec(memory_space=pl.ANY)] * len(deps)
    count = len(args)

    def run(*refs):
        kernel(*refs[:count], *refs[count + len(deps) :])

    return pl.pallas_call(
        run,
        out_shape=[jax.ShapeDtypeStruct(s, d) for s, d in outs],
        in_specs=specs,
        out_specs=[spec(i, far_out) for i in range(len(outs))],
        scratch_shapes=scratch,
        compiler_params=pltpu.CompilerParams(vmem_limit_bytes=limit * 2**20),
        cost_estimate=pl.CostEstimate(
            flops=int(us * 1.15e9), bytes_accessed=2**16, transcendentals=0
        ),
        name=name,
    )(*args, *deps)


def level_start(span, level):
    return span - (span >> (level - 1)) if level else 0


def unit(values):
    centred = values - jnp.mean(values, axis=-1, keepdims=True)
    inv = lax.rsqrt(jnp.mean(centred * centred, axis=-1, keepdims=True) + 1e-05)
    return centred * inv, inv


def unit_back(grad, hat, inv):
    along = jnp.mean(grad * hat, axis=-1, keepdims=True)
    return inv * (grad - jnp.mean(grad, axis=-1, keepdims=True) - hat * along)


def pool_matrix(span):
    parts = []
    for level in range(1, LEVELS):
        rows = span >> level
        row = lax.broadcasted_iota(jnp.int32, (rows, span), 0)
        col = lax.broadcasted_iota(jnp.int32, (rows, span), 1)
        parts.append(jnp.where((col >> level) == row, 1.0 / 2**level, 0.0))
    return jnp.concatenate(parts, axis=0).astype(bf16)


def edge_matrix(span):
    parts = []
    row = lax.broadcasted_iota(jnp.int32, (BLOCK, span), 0)
    col = lax.broadcasted_iota(jnp.int32, (BLOCK, span), 1)
    for level in range(LEVELS):
        group = (span >> level) - BLOCK + row
        parts.append(jnp.where((col >> level) == group, 1.0 / 2**level, 0.0))
    return jnp.concatenate(parts, axis=0).astype(bf16)


def standardize(tokens, hat):
    hat[...] = unit(tokens[...].astype(f32))[0]


def project(hat, gain, bias, w_qkv, normed, queries, kv, coarse, edge):
    span, width = hat.shape
    rows = (hat[...] * gain[...].astype(f32)[None] + bias[...].astype(f32)[None]).astype(bf16)
    normed[...] = rows
    both = nn(rows, w_qkv[:, width:]).astype(bf16)
    kv[...] = both
    pooled = nn(pool_matrix(span), both).astype(bf16)
    coarse[...] = pooled
    edge[0:BLOCK, : 2 * width] = both[span - BLOCK :]
    for level in range(1, LEVELS):
        end = level_start(span, level + 1)
        edge[BLOCK * level : BLOCK * (level + 1), : 2 * width] = pooled[end - BLOCK : end]
    edge[:, 2 * width :] = nn(edge_matrix(span), hat[...].astype(bf16)).astype(bf16)
    q = nn(rows, w_qkv[:, :width]).astype(bf16).astype(f32)
    queries[...] = (q * (1.0 / math.sqrt(width // HEADS))).astype(bf16)


def hidden_back(prefix, cotangent, w_down, d_ffn, d_hidden):
    span, width = cotangent.shape
    position = lax.axis_index("seq") * span + lax.broadcasted_iota(jnp.int32, (span, width), 0)
    masked = jnp.where(position >= prefix[0], cotangent[...].astype(f32), 0.0).astype(bf16)
    d_ffn[...] = masked
    d_hidden[...] = nt(masked, w_down[...])


def window_bias(chunk, first):
    row = lax.broadcasted_iota(jnp.int32, (CHUNK, KEYS), 0)
    col = lax.broadcasted_iota(jnp.int32, (CHUNK, KEYS), 1)
    late = row >= BLOCK
    low = jnp.where(late, BLOCK, 0)
    edge = 3 * BLOCK
    ok = (col >= low) & (col <= BLOCK + row)
    if chunk == 0:
        ok = ok & ((col >= BLOCK) | jnp.logical_not(first))
    bias = jnp.where(ok & (col < edge), 0.0, -1e30)
    for level in range(1, LEVELS):
        start = edge + BLOCK * (level - 1)
        inside = (col >= start) & (col < start + BLOCK)
        half = inside & (col < start + BLOCK // 2)
        if level == 1:
            ok = half | (inside & late)
        else:
            ok = inside if (chunk >> (level - 2)) & 1 else half
        if chunk >> (level - 1) == 0:
            ok = ok & jnp.logical_not(first)
        bias = jnp.where(ok, math.log(2**level), bias)
    return bias


def window_rows(kv, coarse, recv, chunk, low, high, span):
    start = CHUNK * chunk
    if chunk == 0:
        parts = [recv[0:BLOCK, low:high], kv[0:CHUNK, low:high]]
    else:
        parts = [kv[start - BLOCK : start + CHUNK, low:high]]
    for level in range(1, LEVELS):
        block = chunk >> (level - 1)
        if block == 0:
            parts.append(recv[BLOCK * level : BLOCK * (level + 1), low:high])
        else:
            base = level_start(span, level) + BLOCK * (block - 1)
            parts.append(coarse[base : base + BLOCK, low:high])
    return jnp.concatenate(parts, axis=0)


def by_head(rows):
    lane = lax.broadcasted_iota(jnp.int32, (CHUNK, 128), 1)
    zero = jnp.zeros((CHUNK, 128), bf16)
    pairs = []
    for pair in range(HEADS // 2):
        part = rows[:, 128 * pair : 128 * (pair + 1)]
        pairs.append(
            jnp.concatenate(
                [jnp.where(lane < 64, part, zero), jnp.where(lane >= 64, part, zero)], axis=0
            )
        )
    return pairs


def from_heads(pairs):
    lane = lax.broadcasted_iota(jnp.int32, (CHUNK, 128), 1)
    return jnp.concatenate([jnp.where(lane < 64, p[:CHUNK], p[CHUNK:]) for p in pairs], axis=1)


SIDE = 4


def attend(queries, kv, coarse, recv, attended, probs):
    span, width = queries.shape
    first = lax.axis_index("seq") == 0
    rows = CHUNK * HEADS
    for base in range(0, span // CHUNK, SIDE):
        group = range(base, base + SIDE)
        scores = []
        for chunk in group:
            bias = window_bias(chunk, first)
            keys = window_rows(kv, coarse, recv, chunk, 0, width, span)
            split = by_head(queries[CHUNK * chunk : CHUNK * (chunk + 1)])
            raw = [nt(s, keys[:, 128 * p : 128 * (p + 1)]) for p, s in enumerate(split)]
            scores.append(jnp.concatenate(raw, axis=0) + jnp.concatenate([bias] * HEADS, axis=0))
        tops = [jnp.max(s, axis=-1, keepdims=True) for s in scores]
        expos = [jnp.exp(s - t) for s, t in zip(scores, tops)]
        sums = [jnp.sum(e, axis=-1, keepdims=True) for e in expos]
        lows = [(e * (1.0 / t)).astype(bf16) for e, t in zip(expos, sums)]
        for chunk, low in zip(group, lows):
            probs[rows * chunk : rows * (chunk + 1)] = low
            vals = window_rows(kv, coarse, recv, chunk, width, 2 * width, span)
            mixed = [
                nn(low[64 * p : 64 * (p + 1)], vals[:, 128 * p : 128 * (p + 1)])
                for p in range(HEADS // 2)
            ]
            attended[CHUNK * chunk : CHUNK * (chunk + 1)] = from_heads(mixed).astype(bf16)


def core_index():
    return (lax.axis_index("batch") * lax.axis_size("seq") + lax.axis_index("seq")) & 1


def halves(whole, keep, send):
    core = core_index()
    rows = keep.shape[0]
    keep[...] = whole[pl.ds(pl.multiple_of(core * rows, BLOCK), rows)]
    send[...] = whole[pl.ds(pl.multiple_of((1 - core) * rows, BLOCK), rows)]


def feed_forward(
    attended, tokens, w_out, gain, bias, w_up, d_hidden, d_ffn, mid, normed, hidden, d_up, keep, send, whole
):
    span, width = tokens.shape
    ff = w_up.shape[1]
    middle = tokens[...].astype(f32) + nn(attended[...], w_out[...])
    mid[...] = middle
    hat, _ = unit(middle)
    rows = (hat * gain[...].astype(f32)[None] + bias[...].astype(f32)[None]).astype(bf16)
    normed[...] = rows
    c0 = math.sqrt(2.0 / math.pi)
    tile = 256
    for start in range(0, ff, tile):
        cols = slice(start, start + tile)
        x = nn(rows, w_up[:, cols])
        square = x * x
        half = 0.5 + 0.5 * jnp.tanh(x * (c0 + (c0 * 0.044715) * square))
        act = (x * half).astype(bf16)
        slope = half + 2.0 * half * (1.0 - half) * x * (c0 + (3 * c0 * 0.044715) * square)
        hidden[:, cols] = act
        d_up[:, cols] = (slope * d_hidden[:, cols]).astype(bf16)
        whole[cols] = tn(act, d_ffn[...]).astype(bf16)
    halves(whole, keep, send)


def up_back(normed, d_up, keep, send, whole):
    width = normed.shape[1]
    for part in range(d_up.shape[1] // width):
        cols = slice(width * part, width * (part + 1))
        whole[cols] = tn(normed[...], d_up[:, cols]).astype(bf16)
    halves(whole, keep, send)


def mid_back(
    mid, hidden, w_down, d_up, w_up, gain, d_ffn, attended, w_out, out, d_mid, d_attended, keep, send, grad_norm, whole
):
    middle = mid[...]
    out[...] = (middle + nn(hidden[...], w_down[...])).astype(bf16)
    d_normed = nt(d_up[...], w_up[...])
    hat, inv = unit(middle)
    grad_norm[0:1] = jnp.sum(d_normed * hat, axis=0, keepdims=True)
    grad_norm[1:2] = jnp.sum(d_normed, axis=0, keepdims=True)
    d_middle = d_ffn[...].astype(f32) + unit_back(d_normed * gain[...].astype(f32)[None], hat, inv)
    d_mid[...] = d_middle
    d_branch = d_middle.astype(bf16)
    whole[...] = tn(attended[...], d_branch).astype(bf16)
    halves(whole, keep, send)
    d_attended[...] = nt(d_branch, w_out[...]).astype(bf16)


def attend_back(queries, kv, coarse, recv, probs, d_attended, d_proj, lent, fine, wide):
    span, width = queries.shape
    rows = CHUNK * HEADS
    scale = 1.0 / math.sqrt(width // HEADS)
    fine[...] = jnp.zeros_like(fine)
    wide[...] = jnp.zeros_like(wide)
    zero = jnp.zeros((2 * CHUNK, 128), bf16)

    def widened(split, quad):
        return jnp.concatenate(
            [
                jnp.concatenate([split[2 * quad], zero], axis=1),
                jnp.concatenate([zero, split[2 * quad + 1]], axis=1),
            ],
            axis=0,
        )

    for base in range(0, span // CHUNK, SIDE):
        group = range(base, base + SIDE)
        softs, d_probs, splits_a = [], [], []
        for chunk in group:
            vals = window_rows(kv, coarse, recv, chunk, width, 2 * width, span)
            split = by_head(d_attended[CHUNK * chunk : CHUNK * (chunk + 1)])
            splits_a.append(split)
            softs.append(probs[rows * chunk : rows * (chunk + 1)].astype(f32))
            d_probs.append(
                jnp.concatenate(
                    [nt(s, vals[:, 128 * p : 128 * (p + 1)]) for p, s in enumerate(split)], axis=0
                )
            )
        inners = [jnp.sum(s * d, axis=-1, keepdims=True) for s, d in zip(softs, d_probs)]
        d_scores = [(s * (d - t)).astype(bf16) for s, d, t in zip(softs, d_probs, inners)]
        for chunk, d_score, split_a in zip(group, d_scores, splits_a):
            start = CHUNK * chunk
            keys = window_rows(kv, coarse, recv, chunk, 0, width, span)
            mixed = [
                nn(d_score[64 * p : 64 * (p + 1)], keys[:, 128 * p : 128 * (p + 1)])
                for p in range(HEADS // 2)
            ]
            d_proj[start : start + CHUNK, :width] = (from_heads(mixed) * scale).astype(bf16)
            split_q = by_head(queries[start : start + CHUNK])
            low = probs[rows * chunk : rows * (chunk + 1)]
            for part, (left, split) in enumerate(((d_score, split_q), (low, split_a))):
                for quad in range(HEADS // 4):
                    grad = tn(left[128 * quad : 128 * (quad + 1)], widened(split, quad))
                    cols = slice(width * part + 256 * quad, width * part + 256 * (quad + 1))
                    fine[start : start + 3 * BLOCK, cols] += grad[: 3 * BLOCK]
                    for level in range(1, LEVELS):
                        at = level_start(span, level) + BLOCK * (chunk >> (level - 1))
                        own = BLOCK * (level + 2)
                        wide[at : at + BLOCK, cols] += grad[own : own + BLOCK]

    zero = jnp.zeros((BLOCK, 2 * width), bf16)
    lent[0:BLOCK] = fine[0:BLOCK].astype(bf16)
    parts = []
    for level in range(1, LEVELS):
        at, end = level_start(span, level), level_start(span, level + 1)
        lent[BLOCK * level : BLOCK * (level + 1)] = wide[at : at + BLOCK].astype(bf16)
        if at + BLOCK < end:
            parts.append(wide[at + BLOCK : end].astype(bf16))
        parts.append(zero)
    spread = tn(pool_matrix(span), jnp.concatenate(parts, axis=0))
    d_proj[:, width:] = (fine[BLOCK:] + spread).astype(bf16)


def project_back(
    d_proj, lent, recv, normed, w_qkv, tokens, grad_norm, gain, bias, d_normed, keep, send, whole
):
    span, width = tokens.shape
    grads, away = d_proj[...], lent[...]
    gains, shifts = gain[...].astype(f32)[None], bias[...].astype(f32)[None]
    edge_hat = recv[:, 2 * width :].astype(f32)
    edge_normed = (edge_hat * gains + shifts).astype(bf16)
    whole[:, :width] = tn(normed[...], grads[:, :width]).astype(bf16)
    whole[:, width : 3 * width] = (
        tn(normed[...], grads[:, width:]) + tn(edge_normed, away)
    ).astype(bf16)
    d_rows = nt(grads, w_qkv[...])
    d_normed[...] = d_rows
    d_edge = nt(away, w_qkv[:, width:])
    hat, _ = unit(tokens[...].astype(f32))
    small = [
        jnp.sum(d_rows * hat, axis=0, keepdims=True) + jnp.sum(d_edge * edge_hat, axis=0, keepdims=True),
        jnp.sum(d_rows, axis=0, keepdims=True) + jnp.sum(d_edge, axis=0, keepdims=True),
        grad_norm[0:2],
        jnp.zeros((124, width), f32),
    ]
    whole[:, 3 * width :] = jnp.concatenate(small, axis=0).T.astype(bf16)
    halves(whole, keep, send)


def tokens_back(d_normed, back, w_qkv, tokens, gain, d_mid, d_tokens):
    span, width = tokens.shape
    d_edge = nt(back[...], w_qkv[:, width:]).astype(bf16)
    grad = d_normed[...] + tn(edge_matrix(span), d_edge)
    hat, inv = unit(tokens[...].astype(f32))
    d_tokens[...] = (
        d_mid[...] + unit_back(grad * gain[...].astype(f32)[None], hat, inv)
    ).astype(bf16)


def half_of(step, rows, base=0):
    index = lax.axis_index("batch") * lax.axis_size("seq") + lax.axis_index("seq")
    bit = jnp.where((index & 1) == 1, index >> step[1], index >> step[0]) & 1
    here, away = base + bit * rows, base + (1 - bit) * rows
    return pl.ds(pl.multiple_of(here, BLOCK), rows), pl.ds(pl.multiple_of(away, BLOCK), rows)


def add(own, other, total):
    total[...] = own[...] + other[...]


def join(step, parts, own, other, both):
    at = 0
    for rows in parts:
        here, away = half_of(step, rows, 2 * at)
        both[here] = own[at : at + rows]
        both[away] = other[at : at + rows]
        at += rows


def finish_down(own, other, out, tile, sems):
    rows = own.shape[0]
    size = tile.shape[1]
    core = core_index()
    copies = []
    for half, ref in enumerate((own, other)):
        base = (core ^ half) * rows
        for part in range(rows // size):
            slot = half * (rows // size) + part
            tile[slot] = ref[size * part : size * (part + 1)].astype(f32)
            at = pl.ds(pl.multiple_of(base + size * part, size), size)
            copies.append(pltpu.make_async_copy(tile.at[slot], out.at[at], sems.at[slot]))
            copies[-1].start()
    for copy in copies:
        copy.wait()


def finish_up(own, other, out, small, tile, small_tile, sems):
    width, ff = out.shape
    across = ff // width // 2
    rest = small.shape[0] // 2
    core = core_index()
    copies = []
    for half, ref in enumerate((own, other)):
        base = (core ^ half) * across
        for part in range(across):
            slot = half * across + part
            tile[slot] = ref[width * part : width * (part + 1)].astype(f32)
            cols = pl.ds(pl.multiple_of((base + part) * width, width), width)
            copies.append(pltpu.make_async_copy(tile.at[slot], out.at[:, cols], sems.at[slot]))
            copies[-1].start()
        small_tile[half] = ref[width * across :].astype(f32)
        at = pl.ds(pl.multiple_of((core ^ half) * rest, rest), rest)
        copies.append(
            pltpu.make_async_copy(small_tile.at[half], small.at[at], sems.at[2 * across + half])
        )
        copies[-1].start()
    for copy in copies:
        copy.wait()


def finish_rest(own, other, g_qkv, gain1, bias1, gain2, bias2, tile, sems):
    rows = own.shape[0]
    cols = g_qkv.shape[1]
    core = core_index()
    copies = []
    for half, ref in enumerate((own, other)):
        at = pl.ds(pl.multiple_of((core ^ half) * rows, BLOCK), rows)
        tile[half] = ref[:, :cols].astype(f32)
        copies.append(pltpu.make_async_copy(tile.at[half], g_qkv.at[at], sems.at[half]))
        copies[-1].start()
    mine, yours = own[:, cols:].astype(f32), other[:, cols:].astype(f32)
    low = core == 0
    small = jnp.concatenate(
        [jnp.where(low, mine, yours), jnp.where(low, yours, mine)], axis=0
    ).T
    for i, ref in enumerate((gain1, bias1, gain2, bias2)):
        ref[...] = small[i]
    for copy in copies:
        copy.wait()


def flips(size, even, odd):
    return [(i, i ^ (1 << (odd if i & 1 else even))) for i in range(size)]


def add_split(step, *refs):
    parts = (len(refs) - 2) // 2
    keep, send = refs[2 * parts :]
    at = 0
    for own, other in zip(refs[:parts], refs[parts : 2 * parts]):
        rows = own.shape[0] // 2
        here, away = half_of(step, rows)
        send[at : at + rows] = own[away] + other[away]
        keep[at : at + rows] = own[here] + other[here]
        at += rows


class Sum:
    def __init__(self, keep, send, orders, size):
        self.own, self.away = keep, send
        self.parts = [v.shape[0] // 2 for v in keep]
        self.steps = [(0, 0)] + list(zip(*orders))
        self.size = size
        self.at, self.back = 0, False

    def start(self):
        value = self.own if self.back or self.at == len(self.steps) - 1 else self.away
        pairs = flips(self.size, *self.steps[self.at])
        self.other = [lax.ppermute(v, ("batch", "seq"), pairs) for v in value]

    def turn(self, *deps):
        result = self.done(*deps)
        if self.at >= 0:
            self.start()
        return result

    def done(self, *deps):
        own, other = self.own, self.other
        rows, cols = sum(v.shape[0] for v in own), own[0].shape[1]
        last = len(self.steps) - 1
        whole = ((rows, cols), bf16)
        if self.back:
            step = self.steps[self.at]
            self.at -= 1
            if self.at < 0:
                self.own = own[0]
                return other[0]
            parts = self.parts if self.at == 0 else (rows,)
            self.own = call(
                partial(join, step, parts), [((2 * rows, cols), bf16)], *own, *other, deps=deps, name="join"
            )
        elif self.at >= last - 1:
            self.own = call(add, [whole], *own, *other, deps=deps, name="add")
            if self.at == last:
                self.back, self.at = True, last - 1
            else:
                self.at += 1
        else:
            half = ((rows // 2, cols), bf16)
            keep, send = call(
                partial(add_split, self.steps[self.at + 1]), [half, half], *own, *other,
                deps=deps, name="add_split",
            )
            self.own, self.away = [keep], [send]
            self.at += 1
        return self.own[0]


TAIL = "DUDRUDRUDRURDRURDRURDURDUR"


def body(
    tokens, prefix, cotangent, gain1, bias1, w_qkv, w_out, gain2, bias2, w_up, w_down
):
    row_count, span, width = tokens.shape
    ff = w_up.shape[1]
    seq_size, batch_size = lax.axis_size("seq"), lax.axis_size("batch")
    size = seq_size * batch_size
    tokens = tokens.reshape(span, width)
    cotangent = cotangent.reshape(span, width)
    edge_rows = BLOCK * LEVELS
    coarse_rows = level_start(span, LEVELS)
    dma = pltpu.SemaphoreType.DMA
    flat = ((span, width), bf16)
    pair = ((span, 2 * width), bf16)
    pooled = ((coarse_rows, 2 * width), bf16)
    (hat1,) = call(standardize, [((span, width), f32)], tokens, name="standardize", us=3)
    normed1, queries, kv, coarse, edge = call(
        project,
        [flat, flat, pair, pooled, ((edge_rows, 3 * width), bf16)],
        hat1, gain1, bias1, w_qkv, name="project", us=3,
    )
    onward = [(i, (i + 1) % seq_size) for i in range(seq_size)]
    recv = lax.ppermute(edge, "seq", onward)
    d_ffn, d_hidden = call(
        hidden_back, [flat, ((span, ff), f32)], prefix, cotangent, w_down,
        smem=(0,), name="hidden_back",
    )
    attended, probs = call(
        attend,
        [flat, ((span * HEADS, KEYS), bf16)],
        queries, kv, coarse, recv,
        deps=(d_ffn,), name="attend",
    )
    mid, normed2, hidden, d_up, keep_down, send_down = call(
        feed_forward,
        [((span, width), f32), flat, ((span, ff), bf16), ((span, ff), bf16),
         ((ff // 2, width), bf16), ((ff // 2, width), bf16)],
        attended, tokens, w_out, gain2, bias2, w_up, d_hidden, d_ffn,
        scratch=[pltpu.VMEM((ff, width), bf16)], name="feed_forward",
    )
    bits = list(range(1, size.bit_length() - 1))
    one = (bits, bits[1:] + bits[:1])
    two = (bits[1:2] + bits[:1] + bits[2:], bits[:1] + bits[2:] + bits[1:2])
    down = Sum([keep_down], [send_down], one, size)
    down.start()
    half = ((ff // 2, width), bf16)
    keep_up, send_up = call(
        up_back, [half, half], normed2, d_up, scratch=[pltpu.VMEM((ff, width), bf16)], name="up_back",
    )
    step = down.turn(keep_up)
    half = ((width // 2, width), bf16)
    out, d_mid, d_attended, keep_out, send_out, grad_norm = call(
        mid_back,
        [flat, ((span, width), f32), flat, half, half, ((8, width), f32)],
        mid, hidden, w_down, d_up, w_up, gain2, d_ffn, attended, w_out,
        deps=(step,), scratch=[pltpu.VMEM((width, width), bf16)], name="mid_back",
    )
    up = Sum([keep_up, keep_out], [send_up, send_out], two, size)
    up.start()
    step = up.turn(d_attended)
    d_proj, lent = call(
        attend_back,
        [((span, 3 * width), bf16), ((edge_rows, 2 * width), bf16)],
        queries, kv, coarse, recv, probs, d_attended,
        deps=(step,),
        scratch=[pltpu.VMEM((span + BLOCK, 2 * width), f32), pltpu.VMEM((coarse_rows, 2 * width), f32)],
        name="attend_back", limit=16,
    )
    step = down.turn(d_proj)
    half = ((width // 2, 3 * width + 128), bf16)
    d_normed, keep_rest, send_rest = call(
        project_back,
        [((span, width), f32), half, half],
        d_proj, lent, recv, normed1, w_qkv, tokens, grad_norm, gain1, bias1,
        deps=(step,), scratch=[pltpu.VMEM((width, 3 * width + 128), bf16)], name="project_back",
    )
    rest = Sum([keep_rest], [send_rest], one, size)
    rest.start()
    back = lax.ppermute(lent, "seq", [(b, a) for a, b in onward])
    step = up.turn(keep_rest)
    step = rest.turn(step)
    (d_tokens,) = call(
        tokens_back, [flat], d_normed, back, w_qkv, tokens, gain1, d_mid,
        deps=(step,), name="tokens_back",
    )
    step = d_tokens
    ends = {}
    sums = {"D": down, "U": up, "R": rest}
    for key in TAIL * 2:
        if key in ends:
            continue
        step = sums[key].turn(step)
        if sums[key].at < 0:
            ends[key] = (sums[key].own, step)
    tiles = lambda count, rows, cols: pltpu.VMEM((count, rows, cols), f32)
    (grad_down,) = call(
        finish_down, [((ff, width), f32)], *ends["D"], far_out=(0,),
        scratch=[tiles(8, ff // 8, width), dma((8,))], name="finish_down", limit=12,
    )
    grad_up, grad_out = call(
        finish_up, [((width, ff), f32), ((width, width), f32)], *ends["U"], far_out=(0, 1),
        scratch=[tiles(ff // width, width, width), tiles(2, width // 2, width), dma((ff // width + 2,))],
        name="finish_up", limit=12,
    )
    line = ((width,), f32)
    grad_qkv, g_gain1, g_bias1, g_gain2, g_bias2 = call(
        finish_rest, [((width, 3 * width), f32), line, line, line, line],
        *ends["R"], far_out=(0,),
        scratch=[tiles(2, width // 2, 3 * width), dma((2,))],
        name="finish_rest", limit=12,
    )
    shape = (row_count, span, width)
    return (
        out.reshape(shape), d_tokens.reshape(shape), g_gain1, g_bias1, grad_qkv, grad_out,
        g_gain2, g_bias2, grad_up, grad_down,
    )


def solution(mesh):
    placed = (
        P("batch", "seq", None),
        P("batch"),
        P("batch", "seq", None),
        P(),
        P(),
        P(),
        P(),
        P(),
        P(),
        P(),
        P(),
    )
    return jax.shard_map(
        body,
        mesh=mesh,
        in_specs=placed,
        out_specs=(
            P("batch", "seq", None),
            P("batch", "seq", None),
            P(),
            P(),
            P(),
            P(),
            P(),
            P(),
            P(),
            P(),
        ),
        check_vma=False,
    )
```

```python
from functools import partial
import math

import jax
import jax.numpy as jnp
from jax import lax
from jax.experimental import pallas as pl
from jax.experimental.pallas import tpu as pltpu
from jax.sharding import PartitionSpec as P

HEADS = 8
BLOCK = 16
LEVELS = 6
CHUNK = 32
KEYS = 128
f32 = jnp.float32
bf16 = jnp.bfloat16


def nn(a, b):
    return lax.dot_general(a, b, (((1,), (0,)), ((), ())), preferred_element_type=f32)


def nt(a, b):
    return lax.dot_general(a, b, (((1,), (1,)), ((), ())), preferred_element_type=f32)


def tn(a, b):
    return lax.dot_general(a, b, (((0,), (0,)), ((), ())), preferred_element_type=f32)


def call(kernel, outs, *args, scratch=(), smem=(), far=(), far_out=(), deps=(), alias=None, name=None, us=0.5, limit=8):
    def spec(at, apart):
        return pl.BlockSpec(memory_space=pltpu.HBM if at in apart else pltpu.VMEM)

    specs = [
        pl.BlockSpec(memory_space=pltpu.SMEM) if i in smem else spec(i, far) for i in range(len(args))
    ]
    specs += [pl.BlockSpec(memory_space=pl.ANY)] * len(deps)
    count = len(args)
    us = COSTS.get(name, us)

    def run(*refs):
        kernel(*refs[:count], *refs[count + len(deps) :])

    return pl.pallas_call(
        run,
        out_shape=[jax.ShapeDtypeStruct(s, d) for s, d in outs],
        in_specs=specs,
        out_specs=[spec(i, far_out) for i in range(len(outs))],
        scratch_shapes=scratch,
        input_output_aliases=alias or {},
        compiler_params=pltpu.CompilerParams(vmem_limit_bytes=limit * 2**20),
        cost_estimate=pl.CostEstimate(
            flops=int(us * 1.15e9), bytes_accessed=2**16, transcendentals=0
        ),
        name=name,
    )(*args, *deps)


def level_start(span, level):
    return span - (span >> (level - 1)) if level else 0


def unit(values):
    centred = values - jnp.mean(values, axis=-1, keepdims=True)
    inv = lax.rsqrt(jnp.mean(centred * centred, axis=-1, keepdims=True) + 1e-05)
    return centred * inv, inv


def unit_back(grad, hat, inv):
    along = jnp.mean(grad * hat, axis=-1, keepdims=True)
    return inv * (grad - jnp.mean(grad, axis=-1, keepdims=True) - hat * along)


def pool_matrix(span):
    parts = []
    for level in range(1, LEVELS):
        rows = span >> level
        row = lax.broadcasted_iota(jnp.int32, (rows, span), 0)
        col = lax.broadcasted_iota(jnp.int32, (rows, span), 1)
        parts.append(jnp.where((col >> level) == row, 1.0 / 2**level, 0.0))
    return jnp.concatenate(parts, axis=0).astype(bf16)


def edge_matrix(span):
    parts = []
    row = lax.broadcasted_iota(jnp.int32, (BLOCK, span), 0)
    col = lax.broadcasted_iota(jnp.int32, (BLOCK, span), 1)
    for level in range(LEVELS):
        group = (span >> level) - BLOCK + row
        parts.append(jnp.where((col >> level) == group, 1.0 / 2**level, 0.0))
    return jnp.concatenate(parts, axis=0).astype(bf16)


def standardize(tokens, hat):
    hat[...] = unit(tokens[...].astype(f32))[0]


def project(hat, gain, bias, w_qkv, normed, kv, coarse, edge):
    span, width = hat.shape
    rows = (hat[...] * gain[...].astype(f32)[None] + bias[...].astype(f32)[None]).astype(bf16)
    normed[...] = rows
    both = nn(rows, w_qkv[:, width:]).astype(bf16)
    kv[...] = both
    pooled = nn(pool_matrix(span), both).astype(bf16)
    coarse[...] = pooled
    edge[0:BLOCK] = both[span - BLOCK :]
    for level in range(1, LEVELS):
        end = level_start(span, level + 1)
        edge[BLOCK * level : BLOCK * (level + 1)] = pooled[end - BLOCK : end]


def project_q(normed, w_qkv, queries):
    span, width = normed.shape
    q = nn(normed[...], w_qkv[:, :width]).astype(bf16).astype(f32)
    queries[...] = (q * (1.0 / math.sqrt(width // HEADS))).astype(bf16)


def hidden_back(prefix, cotangent, w_down, d_ffn, d_hidden):
    span, width = cotangent.shape
    position = lax.axis_index("seq") * span + lax.broadcasted_iota(jnp.int32, (span, width), 0)
    masked = jnp.where(position >= prefix[0], cotangent[...].astype(f32), 0.0).astype(bf16)
    d_ffn[...] = masked
    d_hidden[...] = nt(masked, w_down[...])


def window_bias(chunk, first):
    row = lax.broadcasted_iota(jnp.int32, (CHUNK, KEYS), 0)
    col = lax.broadcasted_iota(jnp.int32, (CHUNK, KEYS), 1)
    late = row >= BLOCK
    low = jnp.where(late, BLOCK, 0)
    edge = 3 * BLOCK
    ok = (col >= low) & (col <= BLOCK + row)
    if chunk == 0:
        ok = ok & ((col >= BLOCK) | jnp.logical_not(first))
    bias = jnp.where(ok & (col < edge), 0.0, -1e30)
    for level in range(1, LEVELS):
        start = edge + BLOCK * (level - 1)
        inside = (col >= start) & (col < start + BLOCK)
        half = inside & (col < start + BLOCK // 2)
        if level == 1:
            ok = half | (inside & late)
        else:
            ok = inside if (chunk >> (level - 2)) & 1 else half
        if chunk >> (level - 1) == 0:
            ok = ok & jnp.logical_not(first)
        bias = jnp.where(ok, math.log(2**level), bias)
    return bias


def window_rows(kv, coarse, recv, chunk, low, high, span):
    start = CHUNK * chunk
    if chunk == 0:
        parts = [recv[0:BLOCK, low:high], kv[0:CHUNK, low:high]]
    else:
        parts = [kv[start - BLOCK : start + CHUNK, low:high]]
    for level in range(1, LEVELS):
        block = chunk >> (level - 1)
        if block == 0:
            parts.append(recv[BLOCK * level : BLOCK * (level + 1), low:high])
        else:
            base = level_start(span, level) + BLOCK * (block - 1)
            parts.append(coarse[base : base + BLOCK, low:high])
    return jnp.concatenate(parts, axis=0)


def by_head(rows):
    lane = lax.broadcasted_iota(jnp.int32, (CHUNK, 128), 1)
    zero = jnp.zeros((CHUNK, 128), bf16)
    pairs = []
    for pair in range(HEADS // 2):
        part = rows[:, 128 * pair : 128 * (pair + 1)]
        pairs.append(
            jnp.concatenate(
                [jnp.where(lane < 64, part, zero), jnp.where(lane >= 64, part, zero)], axis=0
            )
        )
    return pairs


def from_heads(pairs):
    lane = lax.broadcasted_iota(jnp.int32, (CHUNK, 128), 1)
    return jnp.concatenate([jnp.where(lane < 64, p[:CHUNK], p[CHUNK:]) for p in pairs], axis=1)


SIDE = 8
PIECES = 1


def attend(queries, kv, coarse, recv, hat, attended, probs, edge_hat):
    span, width = queries.shape
    edge_hat[...] = nn(edge_matrix(span), hat[...].astype(bf16)).astype(bf16)
    first = lax.axis_index("seq") == 0
    rows = CHUNK * HEADS
    for base in range(0, span // CHUNK, SIDE):
        group = range(base, base + SIDE)
        scores = []
        for chunk in group:
            bias = window_bias(chunk, first)
            keys = window_rows(kv, coarse, recv, chunk, 0, width, span)
            split = by_head(queries[CHUNK * chunk : CHUNK * (chunk + 1)])
            raw = [nt(s, keys[:, 128 * p : 128 * (p + 1)]) for p, s in enumerate(split)]
            scores.append(jnp.concatenate(raw, axis=0) + jnp.concatenate([bias] * HEADS, axis=0))
        tops = [jnp.max(s, axis=-1, keepdims=True) for s in scores]
        expos = [jnp.exp(s - t) for s, t in zip(scores, tops)]
        sums = [jnp.sum(e, axis=-1, keepdims=True) for e in expos]
        lows = [(e * (1.0 / t)).astype(bf16) for e, t in zip(expos, sums)]
        for chunk, low in zip(group, lows):
            probs[rows * chunk : rows * (chunk + 1)] = low
            vals = window_rows(kv, coarse, recv, chunk, width, 2 * width, span)
            mixed = [
                nn(low[64 * p : 64 * (p + 1)], vals[:, 128 * p : 128 * (p + 1)])
                for p in range(HEADS // 2)
            ]
            attended[CHUNK * chunk : CHUNK * (chunk + 1)] = from_heads(mixed).astype(bf16)


def core_index():
    return (lax.axis_index("batch") * lax.axis_size("seq") + lax.axis_index("seq")) & 1


def halves(whole, keeps, sends):
    core = core_index()
    rows = keeps[0].shape[0]
    for refs, half in ((keeps, core), (sends, 1 - core)):
        base = half * (rows * len(refs))
        for i, ref in enumerate(refs):
            ref[...] = whole[pl.ds(pl.multiple_of(base + rows * i, BLOCK), rows)]


def feed_forward(
    attended, tokens, w_out, gain, bias, w_up, d_hidden, d_ffn, mid, normed, hidden, d_up, keep, send, whole
):
    span, width = tokens.shape
    ff = w_up.shape[1]
    middle = tokens[...].astype(f32) + nn(attended[...], w_out[...])
    mid[...] = middle
    hat, _ = unit(middle)
    rows = (hat * gain[...].astype(f32)[None] + bias[...].astype(f32)[None]).astype(bf16)
    normed[...] = rows
    c0 = math.sqrt(2.0 / math.pi)
    tile = 256
    for start in range(0, ff, tile):
        cols = slice(start, start + tile)
        x = nn(rows, w_up[:, cols])
        square = x * x
        half = 0.5 + 0.5 * jnp.tanh(x * (c0 + (c0 * 0.044715) * square))
        act = (x * half).astype(bf16)
        slope = half + 2.0 * half * (1.0 - half) * x * (c0 + (3 * c0 * 0.044715) * square)
        hidden[:, cols] = act
        d_up[:, cols] = (slope * d_hidden[:, cols]).astype(bf16)
        whole[cols] = tn(act, d_ffn[...]).astype(bf16)
    halves(whole, [keep], [send])


def up_back(normed, d_up, keep, send, whole):
    width = normed.shape[1]
    for part in range(d_up.shape[1] // width):
        cols = slice(width * part, width * (part + 1))
        whole[cols] = tn(normed[...], d_up[:, cols]).astype(bf16)
    halves(whole, [keep], [send])


def output(mid, hidden, w_down, out, token):
    out[...] = (mid[...] + nn(hidden[...], w_down[...])).astype(bf16)
    token[...] = jnp.zeros_like(token)


def mid_back(
    mid, d_up, w_up, gain, d_ffn, attended, w_out, d_mid, d_attended, grad_out, grad_norm
):
    middle = mid[...]
    d_normed = nt(d_up[...], w_up[...])
    hat, inv = unit(middle)
    grad_norm[0:1] = jnp.sum(d_normed * hat, axis=0, keepdims=True)
    grad_norm[1:2] = jnp.sum(d_normed, axis=0, keepdims=True)
    d_middle = d_ffn[...].astype(f32) + unit_back(d_normed * gain[...].astype(f32)[None], hat, inv)
    d_mid[...] = d_middle
    d_branch = d_middle.astype(bf16)
    grad_out[...] = tn(attended[...], d_branch).astype(bf16)
    d_attended[...] = nt(d_branch, w_out[...]).astype(bf16)


def attend_back(queries, kv, coarse, recv, probs, d_attended, d_proj, lent, fine, wide):
    span, width = queries.shape
    rows = CHUNK * HEADS
    scale = 1.0 / math.sqrt(width // HEADS)
    fine[0:BLOCK] = jnp.zeros((BLOCK, 2 * width), f32)
    zero = jnp.zeros((2 * CHUNK, 128), bf16)

    def widened(split, quad):
        return jnp.concatenate(
            [
                jnp.concatenate([split[2 * quad], zero], axis=1),
                jnp.concatenate([zero, split[2 * quad + 1]], axis=1),
            ],
            axis=0,
        )

    for base in range(0, span // CHUNK, SIDE):
        group = range(base, base + SIDE)
        softs, d_probs, splits_a = [], [], []
        for chunk in group:
            vals = window_rows(kv, coarse, recv, chunk, width, 2 * width, span)
            split = by_head(d_attended[CHUNK * chunk : CHUNK * (chunk + 1)])
            splits_a.append(split)
            softs.append(probs[rows * chunk : rows * (chunk + 1)].astype(f32))
            d_probs.append(
                jnp.concatenate(
                    [nt(s, vals[:, 128 * p : 128 * (p + 1)]) for p, s in enumerate(split)], axis=0
                )
            )
        inners = [jnp.sum(s * d, axis=-1, keepdims=True) for s, d in zip(softs, d_probs)]
        d_scores = [(s * (d - t)).astype(bf16) for s, d, t in zip(softs, d_probs, inners)]
        splits_q = []
        for chunk, d_score in zip(group, d_scores):
            start = CHUNK * chunk
            keys = window_rows(kv, coarse, recv, chunk, 0, width, span)
            mixed = [
                nn(d_score[64 * p : 64 * (p + 1)], keys[:, 128 * p : 128 * (p + 1)])
                for p in range(HEADS // 2)
            ]
            d_proj[start : start + CHUNK, :width] = (from_heads(mixed) * scale).astype(bf16)
            splits_q.append(by_head(queries[start : start + CHUNK]))
        for part in range(2):
            for quad in range(HEADS // 4):
                cols = slice(width * part + 256 * quad, width * part + 256 * (quad + 1))
                grads = []
                for chunk, d_score, split_a in zip(group, d_scores, splits_a):
                    if part:
                        left, split = probs[rows * chunk : rows * (chunk + 1)], split_a
                    else:
                        left, split = d_score, splits_q[chunk - base]
                    grads.append(tn(left[128 * quad : 128 * (quad + 1)], widened(split, quad)))
                for i, grad in enumerate(grads):
                    start = CHUNK * (base + i)
                    if i:
                        head = grad[:BLOCK] + grads[i - 1][2 * BLOCK : 3 * BLOCK]
                        fine[start : start + BLOCK, cols] = head
                    else:
                        fine[start : start + BLOCK, cols] += grad[:BLOCK]
                    fine[start + BLOCK : start + 2 * BLOCK, cols] = grad[BLOCK : 2 * BLOCK]
                end = CHUNK * (base + SIDE)
                fine[end : end + BLOCK, cols] = grads[-1][2 * BLOCK : 3 * BLOCK]
                for level in range(1, LEVELS):
                    own = BLOCK * (level + 2)
                    sums = {}
                    for i, grad in enumerate(grads):
                        block = (base + i) >> (level - 1)
                        piece = grad[own : own + BLOCK]
                        sums[block] = sums[block] + piece if block in sums else piece
                    for block, total in sums.items():
                        at = level_start(span, level) + BLOCK * block
                        if base > block << (level - 1):
                            wide[at : at + BLOCK, cols] += total
                        else:
                            wide[at : at + BLOCK, cols] = total

    zero = jnp.zeros((BLOCK, 2 * width), bf16)
    lent[0:BLOCK] = fine[0:BLOCK].astype(bf16)
    parts = []
    for level in range(1, LEVELS):
        at, end = level_start(span, level), level_start(span, level + 1)
        lent[BLOCK * level : BLOCK * (level + 1)] = wide[at : at + BLOCK].astype(bf16)
        if at + BLOCK < end:
            parts.append(wide[at + BLOCK : end].astype(bf16))
        parts.append(zero)
    spread = tn(pool_matrix(span), jnp.concatenate(parts, axis=0))
    d_proj[:, width:] = (fine[BLOCK:] + spread).astype(bf16)


def project_back(
    d_proj, lent, edge_hat, normed, w_qkv, tokens, grad_norm, grad_out, gain, bias, d_normed, edge_back, *refs
):
    span, width = tokens.shape
    keeps, sends, whole = refs[:PIECES], refs[PIECES:-1], refs[-1]
    grads, away = d_proj[...], lent[...]
    gains, shifts = gain[...].astype(f32)[None], bias[...].astype(f32)[None]
    edge = edge_hat[...].astype(f32)
    edge_normed = (edge * gains + shifts).astype(bf16)
    whole[:, :width] = tn(normed[...], grads[:, :width]).astype(bf16)
    whole[:, width : 3 * width] = (
        tn(normed[...], grads[:, width:]) + tn(edge_normed, away)
    ).astype(bf16)
    whole[:, 3 * width : 4 * width] = grad_out[...]
    d_rows = nt(grads, w_qkv[...])
    d_normed[...] = d_rows
    d_edge = nt(away, w_qkv[:, width:])
    edge_back[...] = d_edge.astype(bf16)
    hat, _ = unit(tokens[...].astype(f32))
    small = [
        jnp.sum(d_rows * hat, axis=0, keepdims=True) + jnp.sum(d_edge * edge, axis=0, keepdims=True),
        jnp.sum(d_rows, axis=0, keepdims=True) + jnp.sum(d_edge, axis=0, keepdims=True),
        grad_norm[0:2],
        jnp.zeros((124, width), f32),
    ]
    whole[:, 4 * width :] = jnp.concatenate(small, axis=0).T.astype(bf16)
    halves(whole, keeps, sends)


def spacer(token):
    token[...] = jnp.zeros_like(token)


def tokens_back(d_normed, back, tokens, gain, d_mid, d_tokens, token):
    token[...] = jnp.zeros_like(token)
    span, width = tokens.shape
    grad = d_normed[...] + tn(edge_matrix(span), back[...])
    hat, inv = unit(tokens[...].astype(f32))
    d_tokens[...] = (
        d_mid[...] + unit_back(grad * gain[...].astype(f32)[None], hat, inv)
    ).astype(bf16)


def half_of(step, rows):
    index = lax.axis_index("batch") * lax.axis_size("seq") + lax.axis_index("seq")
    bit = jnp.where((index & 1) == 1, index >> step[1], index >> step[0]) & 1
    here, away = bit * rows, (1 - bit) * rows
    return pl.ds(pl.multiple_of(here, BLOCK), rows), pl.ds(pl.multiple_of(away, BLOCK), rows)


def add(own, other, total):
    total[...] = own[...] + other[...]


def join(step, own, other, both):
    here, away = half_of(step, own.shape[0])
    both[here] = own[...]
    both[away] = other[...]


def write_down(half, mine, *refs):
    out, token, tile, sems = refs[half:]
    rows, size = mine.shape[0], tile.shape[1]
    base = (core_index() ^ half) * rows
    copies = []
    for slot in range(rows // size):
        tile[slot] = mine[size * slot : size * (slot + 1)].astype(f32)
        at = pl.ds(pl.multiple_of(base + size * slot, size), size)
        copies.append(pltpu.make_async_copy(tile.at[slot], out.at[at], sems.at[slot]))
        copies[-1].start()
    token[...] = jnp.zeros_like(token)
    for copy in copies:
        copy.wait()


def write_up(half, mine, *refs):
    out, token, tile, sems = refs[half:]
    width, ff = out.shape
    across, size = ff // width // 2, tile.shape[1]
    base = (core_index() ^ half) * across
    copies = []
    for slot in range(across * width // size):
        part, row = divmod(size * slot, width)
        tile[slot] = mine[size * slot : size * (slot + 1)].astype(f32)
        cols = pl.ds(pl.multiple_of((base + part) * width, width), width)
        copies.append(
            pltpu.make_async_copy(tile.at[slot], out.at[row : row + size, cols], sems.at[slot])
        )
        copies[-1].start()
    token[...] = jnp.zeros_like(token)
    for copy in copies:
        copy.wait()


def write_rest(half, mine, *refs):
    rows = mine.shape[0]
    if half:
        own, refs = refs[0], refs[3:]
        g_qkv, g_out, gain1, bias1, gain2, bias2, token, qkv, out, sems = refs
    else:
        g_qkv, g_out, token, qkv, out, sems = refs
    width = g_out.shape[1]
    size = qkv.shape[1]
    base = (core_index() ^ half) * rows
    copies = []
    for slot in range(rows // size):
        here = slice(size * slot, size * (slot + 1))
        at = pl.ds(pl.multiple_of(base + size * slot, size), size)
        qkv[slot] = mine[here, : 3 * width].astype(f32)
        out[slot] = mine[here, 3 * width : 4 * width].astype(f32)
        for i, (src, dst) in enumerate(((qkv, g_qkv), (out, g_out))):
            copies.append(pltpu.make_async_copy(src.at[slot], dst.at[at], sems.at[2 * slot + i]))
            copies[-1].start()
    token[...] = jnp.zeros_like(token)
    if half:
        ours, theirs = own[:, 4 * width :].astype(f32), mine[:, 4 * width :].astype(f32)
        low = core_index() == 0
        small = jnp.concatenate(
            [jnp.where(low, ours, theirs), jnp.where(low, theirs, ours)], axis=0
        ).T
        for i, ref in enumerate((gain1, bias1, gain2, bias2)):
            ref[...] = small[i]
    for copy in copies:
        copy.wait()


def flips(size, even, odd):
    return [(i, i ^ (1 << (odd if i & 1 else even))) for i in range(size)]


def add_split(step, *refs):
    parts = (len(refs) - 2) // 2
    keep, send = refs[2 * parts :]
    at = 0
    for own, other in zip(refs[:parts], refs[parts : 2 * parts]):
        rows = own.shape[0] // 2
        here, away = half_of(step, rows)
        send[at : at + rows] = own[away] + other[away]
        keep[at : at + rows] = own[here] + other[here]
        at += rows


class Sum:
    def __init__(self, keep, send, orders, size):
        self.own, self.away = keep, send
        self.size = size
        steps = [(0, 0)] + list(zip(*orders))
        rows = sum(v.shape[0] for v in keep)
        self.phases = [("halve", steps[0])]
        for step in steps[1:]:
            if step == steps[-1] or rows < 2 * BLOCK:
                self.phases.append(("whole", step))
            else:
                self.phases.append(("halve", step))
                rows //= 2
        self.phases += [("join", step) for kind, step in reversed(self.phases) if kind == "halve"]
        self.at = 0

    def start(self):
        kind, step = self.phases[self.at]
        value = self.away if kind == "halve" else self.own
        pairs = flips(self.size, *step)
        self.other = [lax.ppermute(v, ("batch", "seq"), pairs) for v in value]

    def turn(self, *deps):
        result = self.done(*deps)
        if self.at < len(self.phases):
            self.start()
        return result

    def left(self):
        return len(self.phases) - self.at

    def done(self, *deps):
        own, other = self.own, self.other
        rows, cols = sum(v.shape[0] for v in own), own[0].shape[1]
        kind, step = self.phases[self.at]
        self.at += 1
        if kind == "join":
            if not self.left():
                return other[0]
            self.own = call(
                partial(join, step), [((2 * rows, cols), bf16)], *own, *other,
                deps=deps, name="join",
            )
        elif self.phases[self.at][0] == "halve":
            half = ((rows // 2, cols), bf16)
            keep, send = call(
                partial(add_split, self.phases[self.at][1]), [half, half], *own, *other,
                deps=deps, name="add_split",
            )
            self.own, self.away = [keep], [send]
        else:
            self.own = call(add, [((rows, cols), bf16)], *own, *other, deps=deps, name="add")
        return self.own[0]


COSTS = {"add_split": 6, "add": 6, "join": 6, "spacer": 10, "mid_back": 0.5, "attend_back": 20, "feed_forward": 1, "project_back": 2, "tokens_back": 20}
PLAN = "ff up - - sD sU D mid U ab pb sR D U R D U U D U R D R D R U D U R D - R U D tb R U ob R R"
ORDERS = {"D": ["xyz", "yxz"], "U": ["xzy", "yxz"], "R": ["xyz", "yxz"]}


def chain_bits(names, size, seq_size):
    seq_bits = seq_size.bit_length() - 1
    last = size.bit_length() - 1
    groups = {
        "y": list(range(1, seq_bits)),
        "x": list(range(seq_bits, min(seq_bits + 1, last))),
        "z": list(range(seq_bits + 1, last)),
        "Z": list(range(seq_bits + 1, last))[::-1],
    }
    return [bit for name in names for bit in groups[name]]


def body(
    tokens, prefix, cotangent, gain1, bias1, w_qkv, w_out, gain2, bias2, w_up, w_down
):
    row_count, span, width = tokens.shape
    ff = w_up.shape[1]
    seq_size, batch_size = lax.axis_size("seq"), lax.axis_size("batch")
    size = seq_size * batch_size
    tokens = tokens.reshape(span, width)
    cotangent = cotangent.reshape(span, width)
    edge_rows = BLOCK * LEVELS
    coarse_rows = level_start(span, LEVELS)
    dma = pltpu.SemaphoreType.DMA
    flat, flat32 = ((span, width), bf16), ((span, width), f32)
    pair = ((span, 2 * width), bf16)
    pooled = ((coarse_rows, 2 * width), bf16)
    edges = ((edge_rows, 2 * width), bf16)
    line = ((width,), f32)
    mark = ((8, 128), f32)

    def tiles(count, rows, cols):
        return pltpu.VMEM((count, rows, cols), f32)

    (hat1,) = call(standardize, [flat32], tokens, name="standardize", us=3)
    normed1, kv, coarse, edge = call(
        project, [flat, pair, pooled, edges], hat1, gain1, bias1, w_qkv, name="project", us=3,
    )
    onward = [(i, (i + 1) % seq_size) for i in range(seq_size)]
    recv = lax.ppermute(edge, "seq", onward)
    (queries,) = call(project_q, [flat], normed1, w_qkv, name="project_q", us=0.1)
    d_ffn, d_hidden = call(
        hidden_back, [flat, ((span, ff), f32)], prefix, cotangent, w_down,
        smem=(0,), deps=(queries,), name="hidden_back", us=0.2,
    )
    attended, probs, edge_hat = call(
        attend,
        [flat, ((span * HEADS, KEYS), bf16), ((edge_rows, width), bf16)],
        queries, kv, coarse, recv, hat1, deps=(d_ffn,), name="attend",
    )
    recv_hat = lax.ppermute(edge_hat, "seq", onward)

    sums, ends, state = {}, {}, {}

    def run_ff(step):
        half = ((ff // 2, width), bf16)
        mid, normed2, hidden, d_up, keep, send = call(
            feed_forward,
            [flat32, flat, ((span, ff), bf16), ((span, ff), bf16), half, half],
            attended, tokens, w_out, gain2, bias2, w_up, d_hidden, d_ffn,
            scratch=[pltpu.VMEM((ff, width), bf16)], name="feed_forward",
        )
        state.update(mid=mid, normed2=normed2, hidden=hidden, d_up=d_up)
        state["D"] = [keep], [send]
        return send

    def run_up(step):
        half = ((ff // 2, width), bf16)
        keep, send = call(
            up_back, [half, half], state["normed2"], state["d_up"],
            deps=(step, recv_hat), scratch=[pltpu.VMEM((ff, width), bf16)], name="up_back",
        )
        state["U"] = [keep], [send]
        return send

    def run_mid(step):
        square = ((width, width), bf16)
        d_mid, d_attended, grad_out, grad_norm = call(
            mid_back,
            [flat32, flat, square, ((8, width), f32)],
            state["mid"], state["d_up"], w_up, gain2, d_ffn, attended, w_out,
            deps=(step,), name="mid_back",
        )
        state.update(d_mid=d_mid, d_attended=d_attended, grad_out=grad_out, grad_norm=grad_norm)
        return d_attended

    def run_ab(step):
        state["d_proj"], lent = call(
            attend_back,
            [((span, 3 * width), bf16), edges],
            queries, kv, coarse, recv, probs, state["d_attended"],
            deps=(step,),
            scratch=[pltpu.VMEM((span + BLOCK, 2 * width), f32), pltpu.VMEM((coarse_rows, 2 * width), f32)],
            name="attend_back", limit=16,
        )
        state["lent"] = lent
        return lent

    def run_pb(step):
        piece = ((width // 2 // PIECES, 4 * width + 128), bf16)
        state["d_normed"], edge_back, *halved = call(
            project_back,
            [flat32, ((edge_rows, width), bf16)] + [piece] * (2 * PIECES),
            state["d_proj"], state["lent"], recv_hat, normed1, w_qkv, tokens, state["grad_norm"], state["grad_out"], gain1, bias1,
            deps=(step,), scratch=[pltpu.VMEM((width, 4 * width + 128), bf16)], name="project_back",
        )
        state["R"] = halved[:PIECES], halved[PIECES:]
        state["back"] = lax.ppermute(edge_back, "seq", [(b, a) for a, b in onward])
        return halved[-1]

    def run_ob(step):
        state["result"], token = call(
            output, [flat, mark], state["mid"], state["hidden"], w_down, deps=(step,), name="output",
        )
        return token

    def run_tb(step):
        state["d_tokens"], token = call(
            tokens_back, [flat, mark], state["d_normed"], state["back"], tokens, gain1, state["d_mid"],
            deps=(step,), name="tokens_back",
        )
        return token

    def finish(key, half, mine, step):
        rows = mine.shape[0]
        if key == "R":
            outs = [((width, 3 * width), f32), ((width, width), f32)]
            size = rows // 4
            scratch = [tiles(4, size, 3 * width), tiles(4, size, width), dma((8,))]
            kernel, small = write_rest, [line] * 4
        else:
            outs = [((ff, width) if key == "D" else (width, ff), f32)]
            scratch = [tiles(4, rows // 4, width), dma((4,))]
            kernel, small = (write_down if key == "D" else write_up), []
        name = {"D": "finish_down", "U": "finish_up", "R": "finish_rest"}[key]
        far_out = tuple(range(len(outs)))
        if half == 0:
            *ends[key], token = call(
                partial(kernel, 0), outs + [mark], mine, far_out=far_out, deps=(step,), scratch=scratch,
                name=name, limit=12,
            )
            return token
        first = list(sums[key].own) if small else []
        before = ends[key]
        at = 1 + len(first)
        *ends[key], token = call(
            partial(kernel, 1), outs + small + [mark], mine, *first, *before,
            far=tuple(range(at, at + len(before))), far_out=far_out, scratch=scratch,
            alias={at + i: i for i in range(len(before))}, name=name, limit=12,
        )
        return token

    kernels = dict(ff=run_ff, up=run_up, mid=run_mid, ab=run_ab, pb=run_pb, ob=run_ob, tb=run_tb)
    def turn(key, step):
        step = sums[key].turn(step)
        if sums[key].left() <= 1:
            step = finish(key, 1 - sums[key].left(), step, step)
        return step

    step = None
    for token in PLAN.split():
        if token == "-":
            (step,) = call(spacer, [mark], deps=(step,), name="spacer", us=100)
        elif token in kernels:
            step = kernels[token](step)
        elif token[0] == "s":
            orders = [chain_bits(names, size, seq_size) for names in ORDERS[token[1]]]
            sums[token[1]] = Sum(*state[token[1]], orders, size)
            sums[token[1]].start()
        else:
            step = turn(token, step)
    while any(one.left() for one in sums.values()):
        for key, one in sums.items():
            if one.left():
                step = turn(key, step)
    (grad_down,) = ends["D"]
    (grad_up,) = ends["U"]
    grad_qkv, grad_out, g_gain1, g_bias1, g_gain2, g_bias2 = ends["R"]
    shape = (row_count, span, width)
    return (
        state["result"].reshape(shape), state["d_tokens"].reshape(shape), g_gain1, g_bias1, grad_qkv,
        grad_out, g_gain2, g_bias2, grad_up, grad_down,
    )


def solution(mesh):
    placed = (
        P("batch", "seq", None),
        P("batch"),
        P("batch", "seq", None),
        P(),
        P(),
        P(),
        P(),
        P(),
        P(),
        P(),
        P(),
    )
    return jax.shard_map(
        body,
        mesh=mesh,
        in_specs=placed,
        out_specs=(
            P("batch", "seq", None),
            P("batch", "seq", None),
            P(),
            P(),
            P(),
            P(),
            P(),
            P(),
            P(),
            P(),
        ),
        check_vma=False,
    )
```

```python
from functools import partial
import math

import jax
import jax.numpy as jnp
from jax import lax
from jax.experimental import pallas as pl
from jax.experimental.pallas import tpu as pltpu
from jax.sharding import PartitionSpec as P

HEADS = 8
BLOCK = 16
LEVELS = 6
CHUNK = 32
KEYS = 128
f32 = jnp.float32
bf16 = jnp.bfloat16


def nn(a, b):
    return lax.dot_general(a, b, (((1,), (0,)), ((), ())), preferred_element_type=f32)


def nt(a, b):
    return lax.dot_general(a, b, (((1,), (1,)), ((), ())), preferred_element_type=f32)


def tn(a, b):
    return lax.dot_general(a, b, (((0,), (0,)), ((), ())), preferred_element_type=f32)


def call(kernel, outs, *args, scratch=(), smem=(), far=(), far_out=(), deps=(), alias=None, name=None, us=0.5, limit=8):
    def spec(at, apart):
        return pl.BlockSpec(memory_space=pltpu.HBM if at in apart else pltpu.VMEM)

    specs = [
        pl.BlockSpec(memory_space=pltpu.SMEM) if i in smem else spec(i, far) for i in range(len(args))
    ]
    specs += [pl.BlockSpec(memory_space=pl.ANY)] * len(deps)
    count = len(args)

    def run(*refs):
        kernel(*refs[:count], *refs[count + len(deps) :])

    return pl.pallas_call(
        run,
        out_shape=[jax.ShapeDtypeStruct(s, d) for s, d in outs],
        in_specs=specs,
        out_specs=[spec(i, far_out) for i in range(len(outs))],
        scratch_shapes=scratch,
        input_output_aliases=alias or {},
        compiler_params=pltpu.CompilerParams(vmem_limit_bytes=limit * 2**20),
        cost_estimate=pl.CostEstimate(
            flops=int(us * 1.15e9), bytes_accessed=2**16, transcendentals=0
        ),
        name=name,
    )(*args, *deps)


def level_start(span, level):
    return span - (span >> (level - 1)) if level else 0


def unit(values):
    centred = values - jnp.mean(values, axis=-1, keepdims=True)
    inv = lax.rsqrt(jnp.mean(centred * centred, axis=-1, keepdims=True) + 1e-05)
    return centred * inv, inv


def unit_back(grad, hat, inv):
    along = jnp.mean(grad * hat, axis=-1, keepdims=True)
    return inv * (grad - jnp.mean(grad, axis=-1, keepdims=True) - hat * along)


def pool_matrix(span):
    parts = []
    for level in range(1, LEVELS):
        rows = span >> level
        row = lax.broadcasted_iota(jnp.int32, (rows, span), 0)
        col = lax.broadcasted_iota(jnp.int32, (rows, span), 1)
        parts.append(jnp.where((col >> level) == row, 1.0 / 2**level, 0.0))
    return jnp.concatenate(parts, axis=0).astype(bf16)


def edge_matrix(span):
    parts = []
    row = lax.broadcasted_iota(jnp.int32, (BLOCK, span), 0)
    col = lax.broadcasted_iota(jnp.int32, (BLOCK, span), 1)
    for level in range(LEVELS):
        group = (span >> level) - BLOCK + row
        parts.append(jnp.where((col >> level) == group, 1.0 / 2**level, 0.0))
    return jnp.concatenate(parts, axis=0).astype(bf16)


def standardize(tokens, hat):
    hat[...] = unit(tokens[...].astype(f32))[0]


def project(hat, gain, bias, w_qkv, normed, kv, coarse, edge):
    span, width = hat.shape
    rows = (hat[...] * gain[...].astype(f32)[None] + bias[...].astype(f32)[None]).astype(bf16)
    normed[...] = rows
    both = nn(rows, w_qkv[:, width:]).astype(bf16)
    kv[...] = both
    pooled = nn(pool_matrix(span), both).astype(bf16)
    coarse[...] = pooled
    edge[0:BLOCK] = both[span - BLOCK :]
    for level in range(1, LEVELS):
        end = level_start(span, level + 1)
        edge[BLOCK * level : BLOCK * (level + 1)] = pooled[end - BLOCK : end]


def project_q(normed, w_qkv, queries):
    span, width = normed.shape
    q = nn(normed[...], w_qkv[:, :width]).astype(bf16).astype(f32)
    queries[...] = (q * (1.0 / math.sqrt(width // HEADS))).astype(bf16)


def hidden_back(prefix, cotangent, w_down, d_ffn, d_hidden):
    span, width = cotangent.shape
    position = lax.axis_index("seq") * span + lax.broadcasted_iota(jnp.int32, (span, width), 0)
    masked = jnp.where(position >= prefix[0], cotangent[...].astype(f32), 0.0).astype(bf16)
    d_ffn[...] = masked
    d_hidden[...] = nt(masked, w_down[...])


def window_bias(chunk, first):
    row = lax.broadcasted_iota(jnp.int32, (CHUNK, KEYS), 0)
    col = lax.broadcasted_iota(jnp.int32, (CHUNK, KEYS), 1)
    late = row >= BLOCK
    low = jnp.where(late, BLOCK, 0)
    edge = 3 * BLOCK
    ok = (col >= low) & (col <= BLOCK + row)
    if chunk == 0:
        ok = ok & ((col >= BLOCK) | jnp.logical_not(first))
    bias = jnp.where(ok & (col < edge), 0.0, -1e30)
    for level in range(1, LEVELS):
        start = edge + BLOCK * (level - 1)
        inside = (col >= start) & (col < start + BLOCK)
        half = inside & (col < start + BLOCK // 2)
        if level == 1:
            ok = half | (inside & late)
        else:
            ok = inside if (chunk >> (level - 2)) & 1 else half
        if chunk >> (level - 1) == 0:
            ok = ok & jnp.logical_not(first)
        bias = jnp.where(ok, math.log(2**level), bias)
    return bias


def window_rows(kv, coarse, recv, chunk, low, high, span):
    start = CHUNK * chunk
    if chunk == 0:
        parts = [recv[0:BLOCK, low:high], kv[0:CHUNK, low:high]]
    else:
        parts = [kv[start - BLOCK : start + CHUNK, low:high]]
    for level in range(1, LEVELS):
        block = chunk >> (level - 1)
        if block == 0:
            parts.append(recv[BLOCK * level : BLOCK * (level + 1), low:high])
        else:
            base = level_start(span, level) + BLOCK * (block - 1)
            parts.append(coarse[base : base + BLOCK, low:high])
    return jnp.concatenate(parts, axis=0)


def by_head(rows):
    lane = lax.broadcasted_iota(jnp.int32, (CHUNK, 128), 1)
    zero = jnp.zeros((CHUNK, 128), bf16)
    pairs = []
    for pair in range(HEADS // 2):
        part = rows[:, 128 * pair : 128 * (pair + 1)]
        pairs.append(
            jnp.concatenate(
                [jnp.where(lane < 64, part, zero), jnp.where(lane >= 64, part, zero)], axis=0
            )
        )
    return pairs


def from_heads(pairs):
    lane = lax.broadcasted_iota(jnp.int32, (CHUNK, 128), 1)
    return jnp.concatenate([jnp.where(lane < 64, p[:CHUNK], p[CHUNK:]) for p in pairs], axis=1)


SIDE = 8
PIECES = 1


def attend(queries, kv, coarse, recv, hat, attended, probs, edge_hat):
    span, width = queries.shape
    edge_hat[...] = nn(edge_matrix(span), hat[...].astype(bf16)).astype(bf16)
    first = lax.axis_index("seq") == 0
    rows = CHUNK * HEADS
    for base in range(0, span // CHUNK, SIDE):
        group = range(base, base + SIDE)
        scores = []
        for chunk in group:
            bias = window_bias(chunk, first)
            keys = window_rows(kv, coarse, recv, chunk, 0, width, span)
            split = by_head(queries[CHUNK * chunk : CHUNK * (chunk + 1)])
            raw = [nt(s, keys[:, 128 * p : 128 * (p + 1)]) for p, s in enumerate(split)]
            scores.append(jnp.concatenate(raw, axis=0) + jnp.concatenate([bias] * HEADS, axis=0))
        tops = [jnp.max(s, axis=-1, keepdims=True) for s in scores]
        expos = [jnp.exp(s - t) for s, t in zip(scores, tops)]
        sums = [jnp.sum(e, axis=-1, keepdims=True) for e in expos]
        lows = [(e * (1.0 / t)).astype(bf16) for e, t in zip(expos, sums)]
        for chunk, low in zip(group, lows):
            probs[rows * chunk : rows * (chunk + 1)] = low
            vals = window_rows(kv, coarse, recv, chunk, width, 2 * width, span)
            mixed = [
                nn(low[64 * p : 64 * (p + 1)], vals[:, 128 * p : 128 * (p + 1)])
                for p in range(HEADS // 2)
            ]
            attended[CHUNK * chunk : CHUNK * (chunk + 1)] = from_heads(mixed).astype(bf16)


def core_index():
    return (lax.axis_index("batch") * lax.axis_size("seq") + lax.axis_index("seq")) & 1


def halves(whole, keeps, sends):
    core = core_index()
    rows = keeps[0].shape[0]
    for refs, half in ((keeps, core), (sends, 1 - core)):
        base = half * (rows * len(refs))
        for i, ref in enumerate(refs):
            ref[...] = whole[pl.ds(pl.multiple_of(base + rows * i, BLOCK), rows)]


def feed_forward(
    attended, tokens, w_out, gain, bias, w_up, d_hidden, d_ffn, mid, normed, hidden, d_up, keep, send, whole
):
    span, width = tokens.shape
    ff = w_up.shape[1]
    middle = tokens[...].astype(f32) + nn(attended[...], w_out[...])
    mid[...] = middle
    hat, _ = unit(middle)
    rows = (hat * gain[...].astype(f32)[None] + bias[...].astype(f32)[None]).astype(bf16)
    normed[...] = rows
    c0 = math.sqrt(2.0 / math.pi)
    tile = 256
    for start in range(0, ff, tile):
        cols = slice(start, start + tile)
        x = nn(rows, w_up[:, cols])
        square = x * x
        half = 0.5 + 0.5 * jnp.tanh(x * (c0 + (c0 * 0.044715) * square))
        act = (x * half).astype(bf16)
        slope = half + 2.0 * half * (1.0 - half) * x * (c0 + (3 * c0 * 0.044715) * square)
        hidden[:, cols] = act
        d_up[:, cols] = (slope * d_hidden[:, cols]).astype(bf16)
        whole[cols] = tn(act, d_ffn[...]).astype(bf16)
    halves(whole, [keep], [send])


def up_back(normed, d_up, keep, send, whole):
    width = normed.shape[1]
    for part in range(d_up.shape[1] // width):
        cols = slice(width * part, width * (part + 1))
        whole[cols] = tn(normed[...], d_up[:, cols]).astype(bf16)
    halves(whole, [keep], [send])


def output(mid, hidden, w_down, out, token):
    out[...] = (mid[...] + nn(hidden[...], w_down[...])).astype(bf16)
    token[...] = jnp.zeros_like(token)


def mid_back(
    mid, d_up, w_up, gain, d_ffn, attended, w_out, d_mid, d_attended, grad_out, grad_norm
):
    middle = mid[...]
    d_normed = nt(d_up[...], w_up[...])
    hat, inv = unit(middle)
    grad_norm[0:1] = jnp.sum(d_normed * hat, axis=0, keepdims=True)
    grad_norm[1:2] = jnp.sum(d_normed, axis=0, keepdims=True)
    d_middle = d_ffn[...].astype(f32) + unit_back(d_normed * gain[...].astype(f32)[None], hat, inv)
    d_mid[...] = d_middle
    d_branch = d_middle.astype(bf16)
    grad_out[...] = tn(attended[...], d_branch).astype(bf16)
    d_attended[...] = nt(d_branch, w_out[...]).astype(bf16)


def attend_back(queries, kv, coarse, recv, probs, d_attended, d_proj, lent, fine, wide):
    span, width = queries.shape
    rows = CHUNK * HEADS
    scale = 1.0 / math.sqrt(width // HEADS)
    fine[0:BLOCK] = jnp.zeros((BLOCK, 2 * width), f32)
    zero = jnp.zeros((2 * CHUNK, 128), bf16)

    def widened(split, quad):
        return jnp.concatenate(
            [
                jnp.concatenate([split[2 * quad], zero], axis=1),
                jnp.concatenate([zero, split[2 * quad + 1]], axis=1),
            ],
            axis=0,
        )

    for base in range(0, span // CHUNK, SIDE):
        group = range(base, base + SIDE)
        softs, d_probs, splits_a = [], [], []
        for chunk in group:
            vals = window_rows(kv, coarse, recv, chunk, width, 2 * width, span)
            split = by_head(d_attended[CHUNK * chunk : CHUNK * (chunk + 1)])
            splits_a.append(split)
            softs.append(probs[rows * chunk : rows * (chunk + 1)].astype(f32))
            d_probs.append(
                jnp.concatenate(
                    [nt(s, vals[:, 128 * p : 128 * (p + 1)]) for p, s in enumerate(split)], axis=0
                )
            )
        inners = [jnp.sum(s * d, axis=-1, keepdims=True) for s, d in zip(softs, d_probs)]
        d_scores = [(s * (d - t)).astype(bf16) for s, d, t in zip(softs, d_probs, inners)]
        splits_q = []
        for chunk, d_score in zip(group, d_scores):
            start = CHUNK * chunk
            keys = window_rows(kv, coarse, recv, chunk, 0, width, span)
            mixed = [
                nn(d_score[64 * p : 64 * (p + 1)], keys[:, 128 * p : 128 * (p + 1)])
                for p in range(HEADS // 2)
            ]
            d_proj[start : start + CHUNK, :width] = (from_heads(mixed) * scale).astype(bf16)
            splits_q.append(by_head(queries[start : start + CHUNK]))
        for part in range(2):
            for quad in range(HEADS // 4):
                cols = slice(width * part + 256 * quad, width * part + 256 * (quad + 1))
                grads = []
                for chunk, d_score, split_a in zip(group, d_scores, splits_a):
                    if part:
                        left, split = probs[rows * chunk : rows * (chunk + 1)], split_a
                    else:
                        left, split = d_score, splits_q[chunk - base]
                    grads.append(tn(left[128 * quad : 128 * (quad + 1)], widened(split, quad)))
                for i, grad in enumerate(grads):
                    start = CHUNK * (base + i)
                    if i:
                        head = grad[:BLOCK] + grads[i - 1][2 * BLOCK : 3 * BLOCK]
                        fine[start : start + BLOCK, cols] = head
                    else:
                        fine[start : start + BLOCK, cols] += grad[:BLOCK]
                    fine[start + BLOCK : start + 2 * BLOCK, cols] = grad[BLOCK : 2 * BLOCK]
                end = CHUNK * (base + SIDE)
                fine[end : end + BLOCK, cols] = grads[-1][2 * BLOCK : 3 * BLOCK]
                for level in range(1, LEVELS):
                    own = BLOCK * (level + 2)
                    sums = {}
                    for i, grad in enumerate(grads):
                        block = (base + i) >> (level - 1)
                        piece = grad[own : own + BLOCK]
                        sums[block] = sums[block] + piece if block in sums else piece
                    for block, total in sums.items():
                        at = level_start(span, level) + BLOCK * block
                        if base > block << (level - 1):
                            wide[at : at + BLOCK, cols] += total
                        else:
                            wide[at : at + BLOCK, cols] = total

    zero = jnp.zeros((BLOCK, 2 * width), bf16)
    lent[0:BLOCK] = fine[0:BLOCK].astype(bf16)
    parts = []
    for level in range(1, LEVELS):
        at, end = level_start(span, level), level_start(span, level + 1)
        lent[BLOCK * level : BLOCK * (level + 1)] = wide[at : at + BLOCK].astype(bf16)
        if at + BLOCK < end:
            parts.append(wide[at + BLOCK : end].astype(bf16))
        parts.append(zero)
    spread = tn(pool_matrix(span), jnp.concatenate(parts, axis=0))
    d_proj[:, width:] = (fine[BLOCK:] + spread).astype(bf16)


def project_back(
    d_proj, lent, edge_hat, normed, w_qkv, tokens, grad_norm, grad_out, gain, bias, d_normed, edge_back, *refs
):
    span, width = tokens.shape
    keeps, sends, whole = refs[:PIECES], refs[PIECES:-1], refs[-1]
    grads, away = d_proj[...], lent[...]
    gains, shifts = gain[...].astype(f32)[None], bias[...].astype(f32)[None]
    edge = edge_hat[...].astype(f32)
    edge_normed = (edge * gains + shifts).astype(bf16)
    whole[:, :width] = tn(normed[...], grads[:, :width]).astype(bf16)
    whole[:, width : 3 * width] = (
        tn(normed[...], grads[:, width:]) + tn(edge_normed, away)
    ).astype(bf16)
    whole[:, 3 * width : 4 * width] = grad_out[...]
    d_rows = nt(grads, w_qkv[...])
    d_normed[...] = d_rows
    d_edge = nt(away, w_qkv[:, width:])
    edge_back[...] = d_edge.astype(bf16)
    hat, _ = unit(tokens[...].astype(f32))
    small = [
        jnp.sum(d_rows * hat, axis=0, keepdims=True) + jnp.sum(d_edge * edge, axis=0, keepdims=True),
        jnp.sum(d_rows, axis=0, keepdims=True) + jnp.sum(d_edge, axis=0, keepdims=True),
        grad_norm[0:2],
        jnp.zeros((124, width), f32),
    ]
    whole[:, 4 * width :] = jnp.concatenate(small, axis=0).T.astype(bf16)
    halves(whole, keeps, sends)


def spacer(token):
    token[...] = jnp.zeros_like(token)


def tokens_back(d_normed, back, tokens, gain, d_mid, d_tokens, token):
    token[...] = jnp.zeros_like(token)
    span, width = tokens.shape
    grad = d_normed[...] + tn(edge_matrix(span), back[...])
    hat, inv = unit(tokens[...].astype(f32))
    d_tokens[...] = (
        d_mid[...] + unit_back(grad * gain[...].astype(f32)[None], hat, inv)
    ).astype(bf16)


def half_of(step, rows):
    index = lax.axis_index("batch") * lax.axis_size("seq") + lax.axis_index("seq")
    bit = jnp.where((index & 1) == 1, index >> step[1], index >> step[0]) & 1
    here, away = bit * rows, (1 - bit) * rows
    return pl.ds(pl.multiple_of(here, BLOCK), rows), pl.ds(pl.multiple_of(away, BLOCK), rows)


def add(own, other, total):
    total[...] = own[...] + other[...]


def join(step, own, other, both):
    here, away = half_of(step, own.shape[0])
    both[here] = own[...]
    both[away] = other[...]


def write_down(half, mine, *refs):
    out, token, tile, sems = refs[half:]
    rows, size = mine.shape[0], tile.shape[1]
    base = (core_index() ^ half) * rows
    copies = []
    for slot in range(rows // size):
        tile[slot] = mine[size * slot : size * (slot + 1)].astype(f32)
        at = pl.ds(pl.multiple_of(base + size * slot, size), size)
        copies.append(pltpu.make_async_copy(tile.at[slot], out.at[at], sems.at[slot]))
        copies[-1].start()
    token[...] = jnp.zeros_like(token)
    for copy in copies:
        copy.wait()


def write_up(half, mine, *refs):
    out, token, tile, sems = refs[half:]
    width, ff = out.shape
    across, size = ff // width // 2, tile.shape[1]
    base = (core_index() ^ half) * across
    copies = []
    for slot in range(across * width // size):
        part, row = divmod(size * slot, width)
        tile[slot] = mine[size * slot : size * (slot + 1)].astype(f32)
        cols = pl.ds(pl.multiple_of((base + part) * width, width), width)
        copies.append(
            pltpu.make_async_copy(tile.at[slot], out.at[row : row + size, cols], sems.at[slot])
        )
        copies[-1].start()
    token[...] = jnp.zeros_like(token)
    for copy in copies:
        copy.wait()


def write_rest(half, mine, *refs):
    rows = mine.shape[0]
    if half:
        own, refs = refs[0], refs[3:]
        g_qkv, g_out, gain1, bias1, gain2, bias2, token, qkv, out, sems = refs
    else:
        g_qkv, g_out, token, qkv, out, sems = refs
    width = g_out.shape[1]
    size = qkv.shape[1]
    base = (core_index() ^ half) * rows
    copies = []
    for slot in range(rows // size):
        here = slice(size * slot, size * (slot + 1))
        at = pl.ds(pl.multiple_of(base + size * slot, size), size)
        qkv[slot] = mine[here, : 3 * width].astype(f32)
        out[slot] = mine[here, 3 * width : 4 * width].astype(f32)
        for i, (src, dst) in enumerate(((qkv, g_qkv), (out, g_out))):
            copies.append(pltpu.make_async_copy(src.at[slot], dst.at[at], sems.at[2 * slot + i]))
            copies[-1].start()
    token[...] = jnp.zeros_like(token)
    if half:
        ours, theirs = own[:, 4 * width :].astype(f32), mine[:, 4 * width :].astype(f32)
        low = core_index() == 0
        small = jnp.concatenate(
            [jnp.where(low, ours, theirs), jnp.where(low, theirs, ours)], axis=0
        ).T
        for i, ref in enumerate((gain1, bias1, gain2, bias2)):
            ref[...] = small[i]
    for copy in copies:
        copy.wait()


def flips(size, even, odd):
    return [(i, i ^ (1 << (odd if i & 1 else even))) for i in range(size)]


def add_split(step, *refs):
    parts = (len(refs) - 2) // 2
    keep, send = refs[2 * parts :]
    at = 0
    for own, other in zip(refs[:parts], refs[parts : 2 * parts]):
        rows = own.shape[0] // 2
        here, away = half_of(step, rows)
        send[at : at + rows] = own[away] + other[away]
        keep[at : at + rows] = own[here] + other[here]
        at += rows


class Sum:
    def __init__(self, keep, send, orders, size):
        self.own, self.away = keep, send
        self.size = size
        steps = [(0, 0)] + list(zip(*orders))
        rows = sum(v.shape[0] for v in keep)
        self.phases = [("halve", steps[0])]
        for step in steps[1:]:
            if step == steps[-1] or rows < 2 * BLOCK:
                self.phases.append(("whole", step))
            else:
                self.phases.append(("halve", step))
                rows //= 2
        self.phases += [("join", step) for kind, step in reversed(self.phases) if kind == "halve"]
        self.at = 0

    def start(self):
        kind, step = self.phases[self.at]
        value = self.away if kind == "halve" else self.own
        pairs = flips(self.size, *step)
        self.other = [lax.ppermute(v, ("batch", "seq"), pairs) for v in value]

    def turn(self, us, *deps):
        result = self.done(us, *deps)
        if self.at < len(self.phases):
            self.start()
        return result

    def left(self):
        return len(self.phases) - self.at

    def done(self, us, *deps):
        own, other = self.own, self.other
        rows, cols = sum(v.shape[0] for v in own), own[0].shape[1]
        kind, step = self.phases[self.at]
        self.at += 1
        if kind == "join":
            if not self.left():
                return other[0]
            self.own = call(
                partial(join, step), [((2 * rows, cols), bf16)], *own, *other,
                deps=deps, name="join", us=us,
            )
        elif self.phases[self.at][0] == "halve":
            half = ((rows // 2, cols), bf16)
            keep, send = call(
                partial(add_split, self.phases[self.at][1]), [half, half], *own, *other,
                deps=deps, name="add_split", us=us,
            )
            self.own, self.away = [keep], [send]
        else:
            self.own = call(add, [((rows, cols), bf16)], *own, *other, deps=deps, name="add", us=us)
        return self.own[0]


PLAN = ["ff", "up", "sD", "-", "sU", "D", "mid", "U", "ab", "pb", "sR", "D", "U", "R", "D", "U", "U", "D", "U", "R", "D", "R", "D", "U", "R", "D", "U", "R", "D", "R", "R", "D", "ob", "U", "U", "tb", "R", "R"]
COSTS = [1, 0.5, 0, 10, 0, 6, 0.5, 6, 20, 2, 0, 6, 6, 6, 8, 6, 8, 6, 6, 6, 6, 6, 8, 6, 6, 6, 6, 6, 6, 40, 6, 6, 0.5, 6, 6, 20, 6, 6]
ORDERS = {"D": ["xyz", "yxz"], "U": ["xzy", "yxz"], "R": ["xyz", "yxz"]}


def chain_bits(names, size, seq_size):
    seq_bits = seq_size.bit_length() - 1
    last = size.bit_length() - 1
    groups = {
        "y": list(range(1, seq_bits)),
        "x": list(range(seq_bits, min(seq_bits + 1, last))),
        "z": list(range(seq_bits + 1, last)),
        "Z": list(range(seq_bits + 1, last))[::-1],
    }
    return [bit for name in names for bit in groups[name]]


def body(
    tokens, prefix, cotangent, gain1, bias1, w_qkv, w_out, gain2, bias2, w_up, w_down
):
    row_count, span, width = tokens.shape
    ff = w_up.shape[1]
    seq_size, batch_size = lax.axis_size("seq"), lax.axis_size("batch")
    size = seq_size * batch_size
    tokens = tokens.reshape(span, width)
    cotangent = cotangent.reshape(span, width)
    edge_rows = BLOCK * LEVELS
    coarse_rows = level_start(span, LEVELS)
    dma = pltpu.SemaphoreType.DMA
    flat, flat32 = ((span, width), bf16), ((span, width), f32)
    pair = ((span, 2 * width), bf16)
    pooled = ((coarse_rows, 2 * width), bf16)
    edges = ((edge_rows, 2 * width), bf16)
    line = ((width,), f32)
    mark = ((8, 128), f32)

    def tiles(count, rows, cols):
        return pltpu.VMEM((count, rows, cols), f32)

    (hat1,) = call(standardize, [flat32], tokens, name="standardize", us=3)
    normed1, kv, coarse, edge = call(
        project, [flat, pair, pooled, edges], hat1, gain1, bias1, w_qkv, name="project", us=3,
    )
    onward = [(i, (i + 1) % seq_size) for i in range(seq_size)]
    recv = lax.ppermute(edge, "seq", onward)
    (queries,) = call(project_q, [flat], normed1, w_qkv, name="project_q", us=0.1)
    d_ffn, d_hidden = call(
        hidden_back, [flat, ((span, ff), f32)], prefix, cotangent, w_down,
        smem=(0,), deps=(queries,), name="hidden_back", us=0.2,
    )
    attended, probs, edge_hat = call(
        attend,
        [flat, ((span * HEADS, KEYS), bf16), ((edge_rows, width), bf16)],
        queries, kv, coarse, recv, hat1, deps=(d_ffn,), name="attend",
    )
    recv_hat = lax.ppermute(edge_hat, "seq", onward)

    sums, ends, state = {}, {}, {}

    def run_ff(step):
        half = ((ff // 2, width), bf16)
        mid, normed2, hidden, d_up, keep, send = call(
            feed_forward,
            [flat32, flat, ((span, ff), bf16), ((span, ff), bf16), half, half],
            attended, tokens, w_out, gain2, bias2, w_up, d_hidden, d_ffn,
            scratch=[pltpu.VMEM((ff, width), bf16)], name="feed_forward", us=state["cost"],
        )
        state.update(mid=mid, normed2=normed2, hidden=hidden, d_up=d_up)
        state["D"] = [keep], [send]
        return send

    def run_up(step):
        half = ((ff // 2, width), bf16)
        keep, send = call(
            up_back, [half, half], state["normed2"], state["d_up"],
            deps=(step, recv_hat), scratch=[pltpu.VMEM((ff, width), bf16)], name="up_back", us=state["cost"],
        )
        state["U"] = [keep], [send]
        return send

    def run_mid(step):
        square = ((width, width), bf16)
        d_mid, d_attended, grad_out, grad_norm = call(
            mid_back,
            [flat32, flat, square, ((8, width), f32)],
            state["mid"], state["d_up"], w_up, gain2, d_ffn, attended, w_out,
            deps=(step,), name="mid_back", us=state["cost"],
        )
        state.update(d_mid=d_mid, d_attended=d_attended, grad_out=grad_out, grad_norm=grad_norm)
        return d_attended

    def run_ab(step):
        state["d_proj"], lent = call(
            attend_back,
            [((span, 3 * width), bf16), edges],
            queries, kv, coarse, recv, probs, state["d_attended"],
            deps=(step,),
            scratch=[pltpu.VMEM((span + BLOCK, 2 * width), f32), pltpu.VMEM((coarse_rows, 2 * width), f32)],
            name="attend_back", us=state["cost"], limit=16,
        )
        state["lent"] = lent
        return lent

    def run_pb(step):
        piece = ((width // 2 // PIECES, 4 * width + 128), bf16)
        state["d_normed"], edge_back, *halved = call(
            project_back,
            [flat32, ((edge_rows, width), bf16)] + [piece] * (2 * PIECES),
            state["d_proj"], state["lent"], recv_hat, normed1, w_qkv, tokens, state["grad_norm"], state["grad_out"], gain1, bias1,
            deps=(step,), scratch=[pltpu.VMEM((width, 4 * width + 128), bf16)], name="project_back", us=state["cost"],
        )
        state["R"] = halved[:PIECES], halved[PIECES:]
        state["back"] = lax.ppermute(edge_back, "seq", [(b, a) for a, b in onward])
        return halved[-1]

    def run_ob(step):
        state["result"], token = call(
            output, [flat, mark], state["mid"], state["hidden"], w_down, deps=(step,), name="output", us=state["cost"],
        )
        return token

    def run_tb(step):
        state["d_tokens"], token = call(
            tokens_back, [flat, mark], state["d_normed"], state["back"], tokens, gain1, state["d_mid"],
            deps=(step,), name="tokens_back", us=state["cost"],
        )
        return token

    def finish(key, half, mine, step):
        rows = mine.shape[0]
        if key == "R":
            outs = [((width, 3 * width), f32), ((width, width), f32)]
            size = rows // 4
            scratch = [tiles(4, size, 3 * width), tiles(4, size, width), dma((8,))]
            kernel, small = write_rest, [line] * 4
        else:
            outs = [((ff, width) if key == "D" else (width, ff), f32)]
            scratch = [tiles(4, rows // 4, width), dma((4,))]
            kernel, small = (write_down if key == "D" else write_up), []
        name = {"D": "finish_down", "U": "finish_up", "R": "finish_rest"}[key]
        far_out = tuple(range(len(outs)))
        if half == 0:
            *ends[key], token = call(
                partial(kernel, 0), outs + [mark], mine, far_out=far_out, deps=(step,), scratch=scratch,
                name=name, us=state["cost"], limit=12,
            )
            return token
        first = list(sums[key].own) if small else []
        before = ends[key]
        at = 1 + len(first)
        *ends[key], token = call(
            partial(kernel, 1), outs + small + [mark], mine, *first, *before,
            far=tuple(range(at, at + len(before))), far_out=far_out, scratch=scratch,
            alias={at + i: i for i in range(len(before))}, name=name, us=state["cost"], limit=12,
        )
        return token

    kernels = dict(ff=run_ff, up=run_up, mid=run_mid, ab=run_ab, pb=run_pb, ob=run_ob, tb=run_tb)
    def turn(key, step):
        step = sums[key].turn(state["cost"], step)
        if sums[key].left() <= 1:
            step = finish(key, 1 - sums[key].left(), step, step)
        return step

    step = None
    for token, cost in zip(PLAN, COSTS):
        state["cost"] = cost
        if token == "-":
            (step,) = call(spacer, [mark], deps=(step,), name="spacer", us=cost)
        elif token in kernels:
            step = kernels[token](step)
        elif token[0] == "s":
            orders = [chain_bits(names, size, seq_size) for names in ORDERS[token[1]]]
            sums[token[1]] = Sum(*state[token[1]], orders, size)
            sums[token[1]].start()
        else:
            step = turn(token, step)
    while any(one.left() for one in sums.values()):
        for key, one in sums.items():
            if one.left():
                step = turn(key, step)
    (grad_down,) = ends["D"]
    (grad_up,) = ends["U"]
    grad_qkv, grad_out, g_gain1, g_bias1, g_gain2, g_bias2 = ends["R"]
    shape = (row_count, span, width)
    return (
        state["result"].reshape(shape), state["d_tokens"].reshape(shape), g_gain1, g_bias1, grad_qkv,
        grad_out, g_gain2, g_bias2, grad_up, grad_down,
    )


def solution(mesh):
    placed = (
        P("batch", "seq", None),
        P("batch"),
        P("batch", "seq", None),
        P(),
        P(),
        P(),
        P(),
        P(),
        P(),
        P(),
        P(),
    )
    return jax.shard_map(
        body,
        mesh=mesh,
        in_specs=placed,
        out_specs=(
            P("batch", "seq", None),
            P("batch", "seq", None),
            P(),
            P(),
            P(),
            P(),
            P(),
            P(),
            P(),
            P(),
        ),
        check_vma=False,
    )
```

```python
from functools import partial
import math

import jax
import jax.numpy as jnp
from jax import lax
from jax.experimental import pallas as pl
from jax.experimental.pallas import tpu as pltpu
from jax.sharding import PartitionSpec as P

HEADS = 8
BLOCK = 16
LEVELS = 6
CHUNK = 32
KEYS = 128
f32 = jnp.float32
bf16 = jnp.bfloat16


def nn(a, b):
    return lax.dot_general(a, b, (((1,), (0,)), ((), ())), preferred_element_type=f32)


def nt(a, b):
    return lax.dot_general(a, b, (((1,), (1,)), ((), ())), preferred_element_type=f32)


def tn(a, b):
    return lax.dot_general(a, b, (((0,), (0,)), ((), ())), preferred_element_type=f32)


def call(kernel, outs, *args, scratch=(), smem=(), far=(), far_out=(), deps=(), alias=None, name=None, us=0.5, limit=8):
    def spec(at, apart):
        return pl.BlockSpec(memory_space=pltpu.HBM if at in apart else pltpu.VMEM)

    specs = [
        pl.BlockSpec(memory_space=pltpu.SMEM) if i in smem else spec(i, far) for i in range(len(args))
    ]
    specs += [pl.BlockSpec(memory_space=pl.ANY)] * len(deps)
    count = len(args)

    def run(*refs):
        kernel(*refs[:count], *refs[count + len(deps) :])

    return pl.pallas_call(
        run,
        out_shape=[jax.ShapeDtypeStruct(s, d) for s, d in outs],
        in_specs=specs,
        out_specs=[spec(i, far_out) for i in range(len(outs))],
        scratch_shapes=scratch,
        input_output_aliases=alias or {},
        compiler_params=pltpu.CompilerParams(vmem_limit_bytes=limit * 2**20),
        cost_estimate=pl.CostEstimate(
            flops=int(us * 1.15e9), bytes_accessed=2**16, transcendentals=0
        ),
        name=name,
    )(*args, *deps)


def level_start(span, level):
    return span - (span >> (level - 1)) if level else 0


def unit(values):
    centred = values - jnp.mean(values, axis=-1, keepdims=True)
    inv = lax.rsqrt(jnp.mean(centred * centred, axis=-1, keepdims=True) + 1e-05)
    return centred * inv, inv


def unit_back(grad, hat, inv):
    along = jnp.mean(grad * hat, axis=-1, keepdims=True)
    return inv * (grad - jnp.mean(grad, axis=-1, keepdims=True) - hat * along)


def pool_matrix(span):
    parts = []
    for level in range(1, LEVELS):
        rows = span >> level
        row = lax.broadcasted_iota(jnp.int32, (rows, span), 0)
        col = lax.broadcasted_iota(jnp.int32, (rows, span), 1)
        parts.append(jnp.where((col >> level) == row, 1.0 / 2**level, 0.0))
    return jnp.concatenate(parts, axis=0).astype(bf16)


def edge_matrix(span):
    parts = []
    row = lax.broadcasted_iota(jnp.int32, (BLOCK, span), 0)
    col = lax.broadcasted_iota(jnp.int32, (BLOCK, span), 1)
    for level in range(LEVELS):
        group = (span >> level) - BLOCK + row
        parts.append(jnp.where((col >> level) == group, 1.0 / 2**level, 0.0))
    return jnp.concatenate(parts, axis=0).astype(bf16)


def standardize(tokens, hat):
    hat[...] = unit(tokens[...].astype(f32))[0]


def project(hat, gain, bias, w_qkv, normed, kv, coarse, edge):
    span, width = hat.shape
    rows = (hat[...] * gain[...].astype(f32)[None] + bias[...].astype(f32)[None]).astype(bf16)
    normed[...] = rows
    both = nn(rows, w_qkv[:, width:]).astype(bf16)
    kv[...] = both
    pooled = nn(pool_matrix(span), both).astype(bf16)
    coarse[...] = pooled
    edge[0:BLOCK] = both[span - BLOCK :]
    for level in range(1, LEVELS):
        end = level_start(span, level + 1)
        edge[BLOCK * level : BLOCK * (level + 1)] = pooled[end - BLOCK : end]


def project_q(normed, w_qkv, queries):
    span, width = normed.shape
    q = nn(normed[...], w_qkv[:, :width]).astype(bf16).astype(f32)
    queries[...] = (q * (1.0 / math.sqrt(width // HEADS))).astype(bf16)


def hidden_back(prefix, cotangent, w_down, d_ffn, d_hidden):
    span, width = cotangent.shape
    position = lax.axis_index("seq") * span + lax.broadcasted_iota(jnp.int32, (span, width), 0)
    masked = jnp.where(position >= prefix[0], cotangent[...].astype(f32), 0.0).astype(bf16)
    d_ffn[...] = masked
    d_hidden[...] = nt(masked, w_down[...])


def window_bias(chunk, first):
    row = lax.broadcasted_iota(jnp.int32, (CHUNK, KEYS), 0)
    col = lax.broadcasted_iota(jnp.int32, (CHUNK, KEYS), 1)
    late = row >= BLOCK
    low = jnp.where(late, BLOCK, 0)
    edge = 3 * BLOCK
    ok = (col >= low) & (col <= BLOCK + row)
    if chunk == 0:
        ok = ok & ((col >= BLOCK) | jnp.logical_not(first))
    bias = jnp.where(ok & (col < edge), 0.0, -1e30)
    for level in range(1, LEVELS):
        start = edge + BLOCK * (level - 1)
        inside = (col >= start) & (col < start + BLOCK)
        half = inside & (col < start + BLOCK // 2)
        if level == 1:
            ok = half | (inside & late)
        else:
            ok = inside if (chunk >> (level - 2)) & 1 else half
        if chunk >> (level - 1) == 0:
            ok = ok & jnp.logical_not(first)
        bias = jnp.where(ok, math.log(2**level), bias)
    return bias


def window_rows(kv, coarse, recv, chunk, low, high, span):
    start = CHUNK * chunk
    if chunk == 0:
        parts = [recv[0:BLOCK, low:high], kv[0:CHUNK, low:high]]
    else:
        parts = [kv[start - BLOCK : start + CHUNK, low:high]]
    for level in range(1, LEVELS):
        block = chunk >> (level - 1)
        if block == 0:
            parts.append(recv[BLOCK * level : BLOCK * (level + 1), low:high])
        else:
            base = level_start(span, level) + BLOCK * (block - 1)
            parts.append(coarse[base : base + BLOCK, low:high])
    return jnp.concatenate(parts, axis=0)


def by_head(rows):
    lane = lax.broadcasted_iota(jnp.int32, (CHUNK, 128), 1)
    zero = jnp.zeros((CHUNK, 128), bf16)
    pairs = []
    for pair in range(HEADS // 2):
        part = rows[:, 128 * pair : 128 * (pair + 1)]
        pairs.append(
            jnp.concatenate(
                [jnp.where(lane < 64, part, zero), jnp.where(lane >= 64, part, zero)], axis=0
            )
        )
    return pairs


def from_heads(pairs):
    lane = lax.broadcasted_iota(jnp.int32, (CHUNK, 128), 1)
    return jnp.concatenate([jnp.where(lane < 64, p[:CHUNK], p[CHUNK:]) for p in pairs], axis=1)


SIDE = 8
PIECES = 1


def attend(queries, kv, coarse, recv, hat, attended, probs, edge_hat):
    span, width = queries.shape
    edge_hat[...] = nn(edge_matrix(span), hat[...].astype(bf16)).astype(bf16)
    first = lax.axis_index("seq") == 0
    rows = CHUNK * HEADS
    for base in range(0, span // CHUNK, SIDE):
        group = range(base, base + SIDE)
        scores = []
        for chunk in group:
            bias = window_bias(chunk, first)
            keys = window_rows(kv, coarse, recv, chunk, 0, width, span)
            split = by_head(queries[CHUNK * chunk : CHUNK * (chunk + 1)])
            raw = [nt(s, keys[:, 128 * p : 128 * (p + 1)]) for p, s in enumerate(split)]
            scores.append(jnp.concatenate(raw, axis=0) + jnp.concatenate([bias] * HEADS, axis=0))
        tops = [jnp.max(s, axis=-1, keepdims=True) for s in scores]
        expos = [jnp.exp(s - t) for s, t in zip(scores, tops)]
        sums = [jnp.sum(e, axis=-1, keepdims=True) for e in expos]
        lows = [(e * (1.0 / t)).astype(bf16) for e, t in zip(expos, sums)]
        for chunk, low in zip(group, lows):
            probs[rows * chunk : rows * (chunk + 1)] = low
            vals = window_rows(kv, coarse, recv, chunk, width, 2 * width, span)
            mixed = [
                nn(low[64 * p : 64 * (p + 1)], vals[:, 128 * p : 128 * (p + 1)])
                for p in range(HEADS // 2)
            ]
            attended[CHUNK * chunk : CHUNK * (chunk + 1)] = from_heads(mixed).astype(bf16)


def core_index():
    return (lax.axis_index("batch") * lax.axis_size("seq") + lax.axis_index("seq")) & 1


def halves(whole, keeps, sends):
    core = core_index()
    rows = keeps[0].shape[0]
    for refs, half in ((keeps, core), (sends, 1 - core)):
        base = half * (rows * len(refs))
        for i, ref in enumerate(refs):
            ref[...] = whole[pl.ds(pl.multiple_of(base + rows * i, BLOCK), rows)]


def feed_forward(
    attended, tokens, w_out, gain, bias, w_up, d_hidden, d_ffn, mid, normed, hidden, d_up, keep, send
):
    span, width = tokens.shape
    ff = w_up.shape[1]
    middle = tokens[...].astype(f32) + nn(attended[...], w_out[...])
    mid[...] = middle
    hat, _ = unit(middle)
    rows = (hat * gain[...].astype(f32)[None] + bias[...].astype(f32)[None]).astype(bf16)
    normed[...] = rows
    c0 = math.sqrt(2.0 / math.pi)
    tile = 256
    core = core_index()
    for half_at, ref in ((core, keep), (1 - core, send)):
        for start in range(0, ff // 2, tile):
            cols = pl.ds(pl.multiple_of(half_at * (ff // 2) + start, tile), tile)
            x = nn(rows, w_up[:, cols])
            square = x * x
            half = 0.5 + 0.5 * jnp.tanh(x * (c0 + (c0 * 0.044715) * square))
            act = (x * half).astype(bf16)
            slope = half + 2.0 * half * (1.0 - half) * x * (c0 + (3 * c0 * 0.044715) * square)
            hidden[:, cols] = act
            d_up[:, cols] = (slope * d_hidden[:, cols]).astype(bf16)
            ref[start : start + tile] = tn(act, d_ffn[...]).astype(bf16)


def up_back(normed, d_up, keep, send):
    width = normed.shape[1]
    core, parts = core_index(), keep.shape[0] // width
    for half_at, ref in ((core, keep), (1 - core, send)):
        for part in range(parts):
            cols = pl.ds(pl.multiple_of((half_at * parts + part) * width, width), width)
            ref[width * part : width * (part + 1)] = tn(normed[...], d_up[:, cols]).astype(bf16)


def output(mid, hidden, w_down, out, token):
    out[...] = (mid[...] + nn(hidden[...], w_down[...])).astype(bf16)
    token[...] = jnp.zeros_like(token)


def mid_back(
    mid, d_up, w_up, gain, d_ffn, attended, w_out, d_mid, d_attended, grad_out, grad_norm
):
    middle = mid[...]
    d_normed = nt(d_up[...], w_up[...])
    hat, inv = unit(middle)
    grad_norm[0:1] = jnp.sum(d_normed * hat, axis=0, keepdims=True)
    grad_norm[1:2] = jnp.sum(d_normed, axis=0, keepdims=True)
    d_middle = d_ffn[...].astype(f32) + unit_back(d_normed * gain[...].astype(f32)[None], hat, inv)
    d_mid[...] = d_middle
    d_branch = d_middle.astype(bf16)
    grad_out[...] = tn(attended[...], d_branch).astype(bf16)
    d_attended[...] = nt(d_branch, w_out[...]).astype(bf16)


def attend_back(queries, kv, coarse, recv, probs, d_attended, d_proj, lent, fine, wide):
    span, width = queries.shape
    rows = CHUNK * HEADS
    scale = 1.0 / math.sqrt(width // HEADS)
    fine[0:BLOCK] = jnp.zeros((BLOCK, 2 * width), f32)
    zero = jnp.zeros((2 * CHUNK, 128), bf16)

    def widened(split, quad):
        return jnp.concatenate(
            [
                jnp.concatenate([split[2 * quad], zero], axis=1),
                jnp.concatenate([zero, split[2 * quad + 1]], axis=1),
            ],
            axis=0,
        )

    for base in range(0, span // CHUNK, SIDE):
        group = range(base, base + SIDE)
        softs, d_probs, splits_a = [], [], []
        for chunk in group:
            vals = window_rows(kv, coarse, recv, chunk, width, 2 * width, span)
            split = by_head(d_attended[CHUNK * chunk : CHUNK * (chunk + 1)])
            splits_a.append(split)
            softs.append(probs[rows * chunk : rows * (chunk + 1)].astype(f32))
            d_probs.append(
                jnp.concatenate(
                    [nt(s, vals[:, 128 * p : 128 * (p + 1)]) for p, s in enumerate(split)], axis=0
                )
            )
        inners = [jnp.sum(s * d, axis=-1, keepdims=True) for s, d in zip(softs, d_probs)]
        d_scores = [(s * (d - t)).astype(bf16) for s, d, t in zip(softs, d_probs, inners)]
        splits_q = []
        for chunk, d_score in zip(group, d_scores):
            start = CHUNK * chunk
            keys = window_rows(kv, coarse, recv, chunk, 0, width, span)
            mixed = [
                nn(d_score[64 * p : 64 * (p + 1)], keys[:, 128 * p : 128 * (p + 1)])
                for p in range(HEADS // 2)
            ]
            d_proj[start : start + CHUNK, :width] = (from_heads(mixed) * scale).astype(bf16)
            splits_q.append(by_head(queries[start : start + CHUNK]))
        for part in range(2):
            for quad in range(HEADS // 4):
                cols = slice(width * part + 256 * quad, width * part + 256 * (quad + 1))
                grads = []
                for chunk, d_score, split_a in zip(group, d_scores, splits_a):
                    if part:
                        left, split = probs[rows * chunk : rows * (chunk + 1)], split_a
                    else:
                        left, split = d_score, splits_q[chunk - base]
                    grads.append(tn(left[128 * quad : 128 * (quad + 1)], widened(split, quad)))
                for i, grad in enumerate(grads):
                    start = CHUNK * (base + i)
                    if i:
                        head = grad[:BLOCK] + grads[i - 1][2 * BLOCK : 3 * BLOCK]
                        fine[start : start + BLOCK, cols] = head
                    else:
                        fine[start : start + BLOCK, cols] += grad[:BLOCK]
                    fine[start + BLOCK : start + 2 * BLOCK, cols] = grad[BLOCK : 2 * BLOCK]
                end = CHUNK * (base + SIDE)
                fine[end : end + BLOCK, cols] = grads[-1][2 * BLOCK : 3 * BLOCK]
                for level in range(1, LEVELS):
                    own = BLOCK * (level + 2)
                    sums = {}
                    for i, grad in enumerate(grads):
                        block = (base + i) >> (level - 1)
                        piece = grad[own : own + BLOCK]
                        sums[block] = sums[block] + piece if block in sums else piece
                    for block, total in sums.items():
                        at = level_start(span, level) + BLOCK * block
                        if base > block << (level - 1):
                            wide[at : at + BLOCK, cols] += total
                        else:
                            wide[at : at + BLOCK, cols] = total

    zero = jnp.zeros((BLOCK, 2 * width), bf16)
    lent[0:BLOCK] = fine[0:BLOCK].astype(bf16)
    parts = []
    for level in range(1, LEVELS):
        at, end = level_start(span, level), level_start(span, level + 1)
        lent[BLOCK * level : BLOCK * (level + 1)] = wide[at : at + BLOCK].astype(bf16)
        if at + BLOCK < end:
            parts.append(wide[at + BLOCK : end].astype(bf16))
        parts.append(zero)
    spread = tn(pool_matrix(span), jnp.concatenate(parts, axis=0))
    d_proj[:, width:] = (fine[BLOCK:] + spread).astype(bf16)


def project_back(
    d_proj, lent, edge_hat, normed, w_qkv, tokens, grad_norm, grad_out, gain, bias, d_normed, edge_back, *refs
):
    span, width = tokens.shape
    keeps, sends, whole = refs[:PIECES], refs[PIECES:-1], refs[-1]
    grads, away = d_proj[...], lent[...]
    gains, shifts = gain[...].astype(f32)[None], bias[...].astype(f32)[None]
    edge = edge_hat[...].astype(f32)
    edge_normed = (edge * gains + shifts).astype(bf16)
    whole[:, :width] = tn(normed[...], grads[:, :width]).astype(bf16)
    whole[:, width : 3 * width] = (
        tn(normed[...], grads[:, width:]) + tn(edge_normed, away)
    ).astype(bf16)
    whole[:, 3 * width : 4 * width] = grad_out[...]
    d_rows = nt(grads, w_qkv[...])
    d_normed[...] = d_rows
    d_edge = nt(away, w_qkv[:, width:])
    edge_back[...] = d_edge.astype(bf16)
    hat, _ = unit(tokens[...].astype(f32))
    small = [
        jnp.sum(d_rows * hat, axis=0, keepdims=True) + jnp.sum(d_edge * edge, axis=0, keepdims=True),
        jnp.sum(d_rows, axis=0, keepdims=True) + jnp.sum(d_edge, axis=0, keepdims=True),
        grad_norm[0:2],
        jnp.zeros((124, width), f32),
    ]
    whole[:, 4 * width :] = jnp.concatenate(small, axis=0).T.astype(bf16)
    halves(whole, keeps, sends)


def spacer(token):
    token[...] = jnp.zeros_like(token)


def tokens_back(d_normed, back, tokens, gain, d_mid, d_tokens, token):
    token[...] = jnp.zeros_like(token)
    span, width = tokens.shape
    grad = d_normed[...] + tn(edge_matrix(span), back[...])
    hat, inv = unit(tokens[...].astype(f32))
    d_tokens[...] = (
        d_mid[...] + unit_back(grad * gain[...].astype(f32)[None], hat, inv)
    ).astype(bf16)


def half_of(step, rows):
    index = lax.axis_index("batch") * lax.axis_size("seq") + lax.axis_index("seq")
    bit = jnp.where((index & 1) == 1, index >> step[1], index >> step[0]) & 1
    here, away = bit * rows, (1 - bit) * rows
    return pl.ds(pl.multiple_of(here, BLOCK), rows), pl.ds(pl.multiple_of(away, BLOCK), rows)


def add(own, other, total):
    total[...] = own[...] + other[...]


def join(step, own, other, both):
    here, away = half_of(step, own.shape[0])
    both[here] = own[...]
    both[away] = other[...]


def write_down(half, mine, *refs):
    out, token, tile, sems = refs[half:]
    rows, size = mine.shape[0], tile.shape[1]
    base = (core_index() ^ half) * rows
    copies = []
    for slot in range(rows // size):
        tile[slot] = mine[size * slot : size * (slot + 1)].astype(f32)
        at = pl.ds(pl.multiple_of(base + size * slot, size), size)
        copies.append(pltpu.make_async_copy(tile.at[slot], out.at[at], sems.at[slot]))
        copies[-1].start()
    token[...] = jnp.zeros_like(token)
    for copy in copies:
        copy.wait()


def write_up(half, mine, *refs):
    out, token, tile, sems = refs[half:]
    width, ff = out.shape
    across, size = ff // width // 2, tile.shape[1]
    base = (core_index() ^ half) * across
    copies = []
    for slot in range(across * width // size):
        part, row = divmod(size * slot, width)
        tile[slot] = mine[size * slot : size * (slot + 1)].astype(f32)
        cols = pl.ds(pl.multiple_of((base + part) * width, width), width)
        copies.append(
            pltpu.make_async_copy(tile.at[slot], out.at[row : row + size, cols], sems.at[slot])
        )
        copies[-1].start()
    token[...] = jnp.zeros_like(token)
    for copy in copies:
        copy.wait()


def write_rest(half, mine, *refs):
    rows = mine.shape[0]
    if half:
        own, refs = refs[0], refs[3:]
        g_qkv, g_out, gain1, bias1, gain2, bias2, token, qkv, out, sems = refs
    else:
        g_qkv, g_out, token, qkv, out, sems = refs
    width = g_out.shape[1]
    size = qkv.shape[1]
    base = (core_index() ^ half) * rows
    copies = []
    for slot in range(rows // size):
        here = slice(size * slot, size * (slot + 1))
        at = pl.ds(pl.multiple_of(base + size * slot, size), size)
        qkv[slot] = mine[here, : 3 * width].astype(f32)
        out[slot] = mine[here, 3 * width : 4 * width].astype(f32)
        for i, (src, dst) in enumerate(((qkv, g_qkv), (out, g_out))):
            copies.append(pltpu.make_async_copy(src.at[slot], dst.at[at], sems.at[2 * slot + i]))
            copies[-1].start()
    token[...] = jnp.zeros_like(token)
    if half:
        ours, theirs = own[:, 4 * width :].astype(f32), mine[:, 4 * width :].astype(f32)
        low = core_index() == 0
        small = jnp.concatenate(
            [jnp.where(low, ours, theirs), jnp.where(low, theirs, ours)], axis=0
        ).T
        for i, ref in enumerate((gain1, bias1, gain2, bias2)):
            ref[...] = small[i]
    for copy in copies:
        copy.wait()


def flips(size, even, odd):
    return [(i, i ^ (1 << (odd if i & 1 else even))) for i in range(size)]


def add_split(step, *refs):
    parts = (len(refs) - 2) // 2
    keep, send = refs[2 * parts :]
    at = 0
    for own, other in zip(refs[:parts], refs[parts : 2 * parts]):
        rows = own.shape[0] // 2
        here, away = half_of(step, rows)
        send[at : at + rows] = own[away] + other[away]
        keep[at : at + rows] = own[here] + other[here]
        at += rows


class Sum:
    def __init__(self, keep, send, orders, size):
        self.own, self.away = keep, send
        self.size = size
        steps = [(0, 0)] + list(zip(*orders))
        rows = sum(v.shape[0] for v in keep)
        self.phases = [("halve", steps[0])]
        for step in steps[1:]:
            if step == steps[-1] or rows < 2 * BLOCK:
                self.phases.append(("whole", step))
            else:
                self.phases.append(("halve", step))
                rows //= 2
        self.phases += [("join", step) for kind, step in reversed(self.phases) if kind == "halve"]
        self.at = 0

    def start(self):
        kind, step = self.phases[self.at]
        value = self.away if kind == "halve" else self.own
        pairs = flips(self.size, *step)
        self.other = [lax.ppermute(v, ("batch", "seq"), pairs) for v in value]

    def turn(self, us, *deps):
        result = self.done(us, *deps)
        if self.at < len(self.phases):
            self.start()
        return result

    def left(self):
        return len(self.phases) - self.at

    def done(self, us, *deps):
        own, other = self.own, self.other
        rows, cols = sum(v.shape[0] for v in own), own[0].shape[1]
        kind, step = self.phases[self.at]
        self.at += 1
        if kind == "join":
            if not self.left():
                return other[0]
            self.own = call(
                partial(join, step), [((2 * rows, cols), bf16)], *own, *other,
                deps=deps, name="join", us=us,
            )
        elif self.phases[self.at][0] == "halve":
            half = ((rows // 2, cols), bf16)
            keep, send = call(
                partial(add_split, self.phases[self.at][1]), [half, half], *own, *other,
                deps=deps, name="add_split", us=us,
            )
            self.own, self.away = [keep], [send]
        else:
            self.own = call(add, [((rows, cols), bf16)], *own, *other, deps=deps, name="add", us=us)
        return self.own[0]


PLAN = ["ff", "up", "sD", "-", "sU", "D", "mid", "U", "ab", "pb", "sR", "D", "U", "R", "D", "U", "U", "D", "U", "R", "D", "R", "D", "U", "R", "D", "U", "R", "D", "R", "R", "D", "ob", "U", "U", "tb", "R", "R"]
COSTS = [1, 0.5, 0, 10, 0, 6, 0.5, 6, 20, 2, 0, 6, 6, 6, 8, 6, 8, 6, 6, 6, 6, 6, 8, 6, 6, 6, 6, 6, 6, 40, 6, 6, 0.5, 6, 6, 20, 6, 6]
ORDERS = {"D": ["xyz", "yxz"], "U": ["xzy", "yxz"], "R": ["xyz", "yxz"]}


def chain_bits(names, size, seq_size):
    seq_bits = seq_size.bit_length() - 1
    last = size.bit_length() - 1
    groups = {
        "y": list(range(1, seq_bits)),
        "x": list(range(seq_bits, min(seq_bits + 1, last))),
        "z": list(range(seq_bits + 1, last)),
        "Z": list(range(seq_bits + 1, last))[::-1],
    }
    return [bit for name in names for bit in groups[name]]


def body(
    tokens, prefix, cotangent, gain1, bias1, w_qkv, w_out, gain2, bias2, w_up, w_down
):
    row_count, span, width = tokens.shape
    ff = w_up.shape[1]
    seq_size, batch_size = lax.axis_size("seq"), lax.axis_size("batch")
    size = seq_size * batch_size
    tokens = tokens.reshape(span, width)
    cotangent = cotangent.reshape(span, width)
    edge_rows = BLOCK * LEVELS
    coarse_rows = level_start(span, LEVELS)
    dma = pltpu.SemaphoreType.DMA
    flat, flat32 = ((span, width), bf16), ((span, width), f32)
    pair = ((span, 2 * width), bf16)
    pooled = ((coarse_rows, 2 * width), bf16)
    edges = ((edge_rows, 2 * width), bf16)
    line = ((width,), f32)
    mark = ((8, 128), f32)

    def tiles(count, rows, cols):
        return pltpu.VMEM((count, rows, cols), f32)

    (hat1,) = call(standardize, [flat32], tokens, name="standardize", us=3)
    normed1, kv, coarse, edge = call(
        project, [flat, pair, pooled, edges], hat1, gain1, bias1, w_qkv, name="project", us=3,
    )
    onward = [(i, (i + 1) % seq_size) for i in range(seq_size)]
    recv = lax.ppermute(edge, "seq", onward)
    (queries,) = call(project_q, [flat], normed1, w_qkv, name="project_q", us=0.1)
    d_ffn, d_hidden = call(
        hidden_back, [flat, ((span, ff), f32)], prefix, cotangent, w_down,
        smem=(0,), deps=(queries,), name="hidden_back", us=0.2,
    )
    attended, probs, edge_hat = call(
        attend,
        [flat, ((span * HEADS, KEYS), bf16), ((edge_rows, width), bf16)],
        queries, kv, coarse, recv, hat1, deps=(d_ffn,), name="attend",
    )
    recv_hat = lax.ppermute(edge_hat, "seq", onward)

    sums, ends, state = {}, {}, {}

    def run_ff(step):
        half = ((ff // 2, width), bf16)
        mid, normed2, hidden, d_up, keep, send = call(
            feed_forward,
            [flat32, flat, ((span, ff), bf16), ((span, ff), bf16), half, half],
            attended, tokens, w_out, gain2, bias2, w_up, d_hidden, d_ffn,
            name="feed_forward", us=state["cost"],
        )
        state.update(mid=mid, normed2=normed2, hidden=hidden, d_up=d_up)
        state["D"] = [keep], [send]
        return send

    def run_up(step):
        half = ((ff // 2, width), bf16)
        keep, send = call(
            up_back, [half, half], state["normed2"], state["d_up"],
            deps=(step, recv_hat), name="up_back", us=state["cost"],
        )
        state["U"] = [keep], [send]
        return send

    def run_mid(step):
        square = ((width, width), bf16)
        d_mid, d_attended, grad_out, grad_norm = call(
            mid_back,
            [flat32, flat, square, ((8, width), f32)],
            state["mid"], state["d_up"], w_up, gain2, d_ffn, attended, w_out,
            deps=(step,), name="mid_back", us=state["cost"],
        )
        state.update(d_mid=d_mid, d_attended=d_attended, grad_out=grad_out, grad_norm=grad_norm)
        return d_attended

    def run_ab(step):
        state["d_proj"], lent = call(
            attend_back,
            [((span, 3 * width), bf16), edges],
            queries, kv, coarse, recv, probs, state["d_attended"],
            deps=(step,),
            scratch=[pltpu.VMEM((span + BLOCK, 2 * width), f32), pltpu.VMEM((coarse_rows, 2 * width), f32)],
            name="attend_back", us=state["cost"], limit=16,
        )
        state["lent"] = lent
        return lent

    def run_pb(step):
        piece = ((width // 2 // PIECES, 4 * width + 128), bf16)
        state["d_normed"], edge_back, *halved = call(
            project_back,
            [flat32, ((edge_rows, width), bf16)] + [piece] * (2 * PIECES),
            state["d_proj"], state["lent"], recv_hat, normed1, w_qkv, tokens, state["grad_norm"], state["grad_out"], gain1, bias1,
            deps=(step,), scratch=[pltpu.VMEM((width, 4 * width + 128), bf16)], name="project_back", us=state["cost"],
        )
        state["R"] = halved[:PIECES], halved[PIECES:]
        state["back"] = lax.ppermute(edge_back, "seq", [(b, a) for a, b in onward])
        return halved[-1]

    def run_ob(step):
        state["result"], token = call(
            output, [flat, mark], state["mid"], state["hidden"], w_down, deps=(step,), name="output", us=state["cost"],
        )
        return token

    def run_tb(step):
        state["d_tokens"], token = call(
            tokens_back, [flat, mark], state["d_normed"], state["back"], tokens, gain1, state["d_mid"],
            deps=(step,), name="tokens_back", us=state["cost"],
        )
        return token

    def finish(key, half, mine, step):
        rows = mine.shape[0]
        if key == "R":
            outs = [((width, 3 * width), f32), ((width, width), f32)]
            size = rows // 4
            scratch = [tiles(4, size, 3 * width), tiles(4, size, width), dma((8,))]
            kernel, small = write_rest, [line] * 4
        else:
            outs = [((ff, width) if key == "D" else (width, ff), f32)]
            scratch = [tiles(4, rows // 4, width), dma((4,))]
            kernel, small = (write_down if key == "D" else write_up), []
        name = {"D": "finish_down", "U": "finish_up", "R": "finish_rest"}[key]
        far_out = tuple(range(len(outs)))
        if half == 0:
            *ends[key], token = call(
                partial(kernel, 0), outs + [mark], mine, far_out=far_out, deps=(step,), scratch=scratch,
                name=name, us=state["cost"], limit=12,
            )
            return token
        first = list(sums[key].own) if small else []
        before = ends[key]
        at = 1 + len(first)
        *ends[key], token = call(
            partial(kernel, 1), outs + small + [mark], mine, *first, *before,
            far=tuple(range(at, at + len(before))), far_out=far_out, scratch=scratch,
            alias={at + i: i for i in range(len(before))}, name=name, us=state["cost"], limit=12,
        )
        return token

    kernels = dict(ff=run_ff, up=run_up, mid=run_mid, ab=run_ab, pb=run_pb, ob=run_ob, tb=run_tb)
    def turn(key, step):
        step = sums[key].turn(state["cost"], step)
        if sums[key].left() <= 1:
            step = finish(key, 1 - sums[key].left(), step, step)
        return step

    step = None
    for token, cost in zip(PLAN, COSTS):
        state["cost"] = cost
        if token == "-":
            (step,) = call(spacer, [mark], deps=(step,), name="spacer", us=cost)
        elif token in kernels:
            step = kernels[token](step)
        elif token[0] == "s":
            orders = [chain_bits(names, size, seq_size) for names in ORDERS[token[1]]]
            sums[token[1]] = Sum(*state[token[1]], orders, size)
            sums[token[1]].start()
        else:
            step = turn(token, step)
    while any(one.left() for one in sums.values()):
        for key, one in sums.items():
            if one.left():
                step = turn(key, step)
    (grad_down,) = ends["D"]
    (grad_up,) = ends["U"]
    grad_qkv, grad_out, g_gain1, g_bias1, g_gain2, g_bias2 = ends["R"]
    shape = (row_count, span, width)
    return (
        state["result"].reshape(shape), state["d_tokens"].reshape(shape), g_gain1, g_bias1, grad_qkv,
        grad_out, g_gain2, g_bias2, grad_up, grad_down,
    )


def solution(mesh):
    placed = (
        P("batch", "seq", None),
        P("batch"),
        P("batch", "seq", None),
        P(),
        P(),
        P(),
        P(),
        P(),
        P(),
        P(),
        P(),
    )
    return jax.shard_map(
        body,
        mesh=mesh,
        in_specs=placed,
        out_specs=(
            P("batch", "seq", None),
            P("batch", "seq", None),
            P(),
            P(),
            P(),
            P(),
            P(),
            P(),
            P(),
            P(),
        ),
        check_vma=False,
    )
```
